128 devices in a mesh: rep: 4 (over y), dp: 32 (over z, x, core).
Axes of the slice: x: 4, y: 4, z: 4, core: 2. Of those that a mesh axis runs over, the one named last changes fastest.
Arguments:
- gradient: bfloat16 [4, 64, 512, 512], P('rep', None, 'dp')
- owner: int32 [64, 1], replicated, may hold values from 0 to 31; in each aligned block of 64 rows (0 to 63, 64 to 127, ...) at most 4 rows name the same one
- left_factor: float32 [128, 512, 512], P('dp'), as said below
- right_factor: float32 [128, 512, 512], P('dp'), as said below
- left_root: bfloat16 [128, 512, 512], P('dp'), as said below
- right_root: bfloat16 [128, 512, 512], P('dp'), as said below
Outputs:
- update: bfloat16 [64, 512, 512], P(None, 'dp')
- left_out: float32 [128, 512, 512], P('dp')
- right_out: float32 [128, 512, 512], P('dp')
The draws below stay inside these ranges and needn't reach their ends.
Inputs may be any that keep to these rules, and one draw needn't show every extreme that they name: `owner`: every dp index owns 1 to 4 blocks and some index owns exactly 4. `left_factor`: symmetric in the last two dimensions. `right_factor`: symmetric in the last two dimensions. `left_root`: symmetric in the last two dimensions. `right_root`: symmetric in the last two dimensions.
All inputs are finite; a program needn't handle non-finite values.
Results may differ from the reference program's by a relative error of at most 0.018.
Values may be sent and summed in bfloat16 or wider, within the bound.
A program may use at most 128 MiB of HBM per device.

```python
import math
import jax
import jax.numpy as jnp
import numpy as np
from jax import lax

BLOCK = 512
CAP = 4
BLOCKS = 64
SLOTS = 128
N_REP = 4
N_DP = 32


def settle(key, noise, low, high):
    diag = jnp.exp(jax.random.uniform(key, (SLOTS, BLOCK), jnp.float32, math.log(low), math.log(high)))
    off = (noise + jnp.swapaxes(noise, 1, 2)) * (0.5 / math.sqrt(BLOCK))
    eye = jnp.eye(BLOCK, dtype=jnp.float32)
    return off + eye[None, :, :] * diag[:, :, None]


def draw_gradient(key, part):
    key = jax.random.fold_in(key, 11)
    first, second, third = jax.random.split(key, 3)
    rows = jnp.exp(jax.random.uniform(first, (BLOCKS, BLOCK, 1), jnp.float32, 0.0, math.log(3.2)))
    cols = jnp.exp(jax.random.uniform(second, (BLOCKS, 1, BLOCK), jnp.float32, 0.0, math.log(3.2)))
    values = jax.random.normal(third, (N_REP, BLOCKS, BLOCK, BLOCK), jnp.float32)
    return (values * rows * cols * 0.12).astype(jnp.bfloat16)


def draw_left_factor(key, part):
    key = jax.random.fold_in(key, 21)
    first, second = jax.random.split(key)
    noise = jax.random.normal(second, (SLOTS, BLOCK, BLOCK), jnp.float32)
    return settle(first, noise, 0.5, 2.0).astype(jnp.float32)


def draw_right_factor(key, part):
    key = jax.random.fold_in(key, 22)
    first, second = jax.random.split(key)
    noise = jax.random.normal(second, (SLOTS, BLOCK, BLOCK), jnp.float32)
    return settle(first, noise, 0.5, 2.0).astype(jnp.float32)


def draw_left_root(key, part):
    key = jax.random.fold_in(key, 23)
    first, second = jax.random.split(key)
    noise = jax.random.normal(second, (SLOTS, BLOCK, BLOCK), jnp.float32)
    return settle(first, noise, 0.8, 1.6).astype(jnp.bfloat16)


def draw_right_root(key, part):
    key = jax.random.fold_in(key, 24)
    first, second = jax.random.split(key)
    noise = jax.random.normal(second, (SLOTS, BLOCK, BLOCK), jnp.float32)
    return settle(first, noise, 0.8, 1.6).astype(jnp.bfloat16)


def routed_block(rng, own, number, rows, amount, top, bound, slope):
    order = jax.random.permutation(rng, amount)
    packed, usual = load_shares(amount, rows * top, bound, slope, True), load_shares(amount, rows * top, bound, slope, False)
    places = jnp.arange(amount)

    def named(sizes, rotation):
        used = int((sizes > 0).sum())
        fixed = max(1, used // 4)
        moved = fixed + (places - fixed + rotation * (used - fixed)) % max(1, amount - fixed)
        return jnp.zeros((amount,), jnp.int32).at[order[jnp.where(places < fixed, places, moved)]].set(jnp.asarray(sizes, jnp.int32))

    sizes = jnp.where(number % 4 == 0, named(packed, number // 4), named(usual, number - number // 4 - 1))
    mixed = jax.random.permutation(jax.random.fold_in(own, 3), amount)
    donor, sink = mixed[0:amount // 2 * 2:2], mixed[1:amount // 2 * 2:2]
    slack = jnp.minimum(sizes[donor] - 1, bound - sizes[sink]) // 2
    slack = jnp.where((donor == order[0]) | (sink == order[0]) | (sizes[sink] == 0), 0, jnp.maximum(slack, 0))
    moved = jax.random.randint(jax.random.fold_in(own, 4), (amount // 2,), 0, 1 << 20) % (slack + 1)
    sizes = sizes.at[donor].add(-moved).at[sink].add(moved)
    members = jnp.searchsorted(jnp.cumsum(sizes), jnp.arange(rows * top), side="right").astype(jnp.int32)
    grid = members.reshape(top, rows).T
    grid = grid[jax.random.permutation(jax.random.fold_in(own, 1), rows)]
    rotation = jax.random.randint(jax.random.fold_in(own, 2), (rows, 1), 0, top)
    return jnp.take_along_axis(grid, (jnp.arange(top)[None, :] + rotation) % top, axis=1)


def load_shares(number_of, total, limit, slope, full):
    portions = [(1 << 20) // math.isqrt(rank ** slope) + 1 for rank in range(1, number_of + 1)]
    largest = limit if full else min(limit, max(-(-total // number_of), total * portions[0] // sum(portions)))
    least = 1 if total - largest >= number_of - 1 else 0
    given, rest = [largest] + [least] * (number_of - 1), total - largest - least * (number_of - 1)
    while rest > 0:
        movable = [i for i in range(1, number_of) if given[i] < largest] or [i for i in range(1, number_of) if given[i] < limit]
        pool, budget = sum([portions[i] for i in movable]), rest
        for i in movable:
            extra = min(limit - given[i], max(1, budget * portions[i] // pool), rest)
            given[i] = given[i] + extra
            rest = rest - extra
    return np.array(given)


def setup_inputs(seed: int = 0) -> dict:
    key_of = jax.random.split(jax.random.key(seed), 7)
    gradient = draw_gradient(jax.random.fold_in(key_of[6], 71), 0)
    owner_keys = jax.random.split(jax.random.fold_in(key_of[1], 1), BLOCKS // BLOCKS)
    owner_turns = jax.random.permutation(jax.random.fold_in(key_of[1], 3), BLOCKS // BLOCKS)
    owner = jax.vmap(lambda own, number: routed_block(jax.random.fold_in(key_of[1], 2), own, number, BLOCKS, N_DP, 1, CAP, 1))(owner_keys, owner_turns).reshape((BLOCKS, 1))
    left_factor = draw_left_factor(jax.random.fold_in(key_of[6], 71), 0)
    right_factor = draw_right_factor(jax.random.fold_in(key_of[6], 71), 0)
    left_root = draw_left_root(jax.random.fold_in(key_of[6], 71), 0)
    right_root = draw_right_root(jax.random.fold_in(key_of[6], 71), 0)
    return {"gradient": gradient, "owner": owner, "left_factor": left_factor, "right_factor": right_factor, "left_root": left_root, "right_root": right_root}


DECAY = 0.9
EPS = 1e-06

def reference(gradient, owner, left_factor, right_factor, left_root, right_root):
    owners = owner[:, 0].astype(jnp.int32)
    position = jnp.arange(BLOCKS, dtype=jnp.int32)
    same = owners[:, None] == owners[None, :]
    earlier = position[None, :] < position[:, None]
    slot = lax.optimization_barrier(jnp.sum((same & earlier).astype(jnp.int32), axis=1)).astype(jnp.int32)
    index = (owners * CAP + slot).astype(jnp.int32)
    summed = lax.optimization_barrier(jnp.sum(gradient.astype(jnp.float32), axis=0))
    high = lax.Precision.HIGHEST
    left_new = DECAY * left_factor[index] + (1.0 - DECAY) / BLOCK * jnp.einsum('bij,bkj->bik', summed, summed, precision=high)
    right_new = DECAY * right_factor[index] + (1.0 - DECAY) / BLOCK * jnp.einsum('bji,bjk->bik', summed, summed, precision=high)
    left_out = (DECAY * left_factor).at[index].set(left_new)
    right_out = (DECAY * right_factor).at[index].set(right_new)
    grad_low = summed.astype(jnp.bfloat16)
    half = jnp.einsum('bij,bjk->bik', left_root[index].astype(jnp.float32), grad_low.astype(jnp.float32), precision=high).astype(jnp.bfloat16)
    direction = jnp.einsum('bij,bjk->bik', half.astype(jnp.float32), right_root[index].astype(jnp.float32), precision=high)
    grad_norm = jnp.sqrt(lax.optimization_barrier(jnp.sum(summed * summed, axis=(1, 2), keepdims=True)))
    dir_norm = jnp.sqrt(lax.optimization_barrier(jnp.sum(direction * direction, axis=(1, 2), keepdims=True)) + EPS)
    update = (direction * (grad_norm / dir_norm)).astype(jnp.bfloat16)
    return (update, left_out, right_out)
```

```python
import functools

import jax
import jax.numpy as jnp
from jax import lax
from jax.experimental import pallas as pl
from jax.experimental.pallas import tpu as pltpu
from jax.sharding import PartitionSpec as P

MESH = pl.DeviceIdType.MESH
CAP = 4
DECAY = 0.9
EPS = 1e-06
CHUNKS = 2
STEPS = (1, 3, 2)
TAB_ROWS = 16
ROW_BLOCK, ROW_POS, ROW_OWNER, ROW_START, ROW_COUNT, ROW_PLACE = 0, 1, 2, 3, 4, 5


def in_vmem(shape, dtype):
    return pltpu.VMEM(shape, dtype)


def from_vmem(x):
    return pltpu.with_memory_space_constraint(x, pltpu.VMEM)


def fill_tables(owner_ref, tab_ref):
    blocks = owner_ref.shape[1]
    lanes = tab_ref.shape[1]
    b = lax.broadcasted_iota(jnp.int32, (blocks, lanes), 0)
    c = lax.broadcasted_iota(jnp.int32, (blocks, lanes), 1)

    def down(x):
        return jnp.sum(x, axis=0, keepdims=True)

    inside = c < blocks
    row = jnp.broadcast_to(jnp.pad(owner_ref[...], ((0, 0), (0, lanes - blocks))), (blocks, lanes))
    col = jnp.sum(jnp.where(b == c, row, 0), axis=1, keepdims=True)
    col = jnp.broadcast_to(col, (blocks, lanes))
    before = (row < col) | ((row == col) & (c < b))
    pos_col = jnp.sum(jnp.where(before & inside, 1, 0), axis=1, keepdims=True)
    pos_col = jnp.broadcast_to(pos_col, (blocks, lanes))
    after = (col < row) | ((col == row) & (b < c))
    pos_row = down(jnp.where(after, 1, 0))
    here = pos_col == c
    start = down(jnp.where(col < c, 1, 0))
    count = down(jnp.where(col == c, 1, 0))
    tab_ref[ROW_BLOCK : ROW_BLOCK + 1, :] = down(jnp.where(here, b, 0))
    tab_ref[ROW_POS : ROW_POS + 1, :] = pos_row
    tab_ref[ROW_OWNER : ROW_OWNER + 1, :] = down(jnp.where(here, col, 0))
    tab_ref[ROW_START : ROW_START + 1, :] = start
    tab_ref[ROW_COUNT : ROW_COUNT + 1, :] = count
    for q in range(CAP):
        slot = (q - start) & 3
        place = jnp.where(slot < count, (start + slot) >> 2, 0)
        tab_ref[ROW_PLACE + q : ROW_PLACE + q + 1, :] = place
    rest = ROW_PLACE + CAP
    tab_ref[rest:, :] = jnp.zeros((TAB_ROWS - rest, lanes), jnp.int32)


def exchange(
    reps, devs, owner_ref, grad_hbm, lf_hbm, rf_hbm, lr_hbm, rr_hbm,
    tab_out, gath, uall, lf_out, rf_out,
    tab, grad, lroot, rroot, rs_send, rs_recv, stage, half, direct, upd, s_own, s_recv, back,
    loc_sem, rs_ss, rs_rs, ag_ss, ag_rs, pr_ss, pr_rs, ot_ss, ot_rs, bk_ss, bk_rs, au_ss, au_rs,
):
    r = lax.axis_index("rep")
    d = lax.axis_index("dp")
    places, rows, width = s_own[0].shape[0], grad.shape[1], grad.shape[2]
    part = width // CHUNKS
    cols = [pl.ds(c * part, part) for c in range(CHUNKS)]
    tile = min(256, width)
    mine = pl.ds(pl.multiple_of(d * rows, rows), rows)

    def rep_peer(k):
        return (lax.rem(r + k, reps), d)

    def dp_peer(t):
        return lax.rem(d + t, devs)

    def local(src, dst, i):
        return pltpu.make_async_copy(src, dst, loc_sem.at[i])

    loads = [
        local(grad_hbm, grad, 0),
        local(lr_hbm, lroot, 1),
        local(rr_hbm, rroot, 2),
        local(lf_hbm, lf_out, 3),
        local(rf_hbm, rf_out, 4),
    ]
    for load in loads:
        load.start()

    barrier = pltpu.get_barrier_semaphore()
    for k in STEPS:
        pl.semaphore_signal(barrier, inc=1, device_id=rep_peer(k), device_id_type=MESH)

    def greet(t, carry):
        pl.semaphore_signal(barrier, inc=1, device_id=(r, dp_peer(t)), device_id_type=MESH)
        return carry

    lax.fori_loop(1, devs, greet, 0)

    fill_tables(owner_ref, tab_out)
    to_scalars = local(tab_out, tab, 5)
    to_scalars.start()
    to_scalars.wait()
    loads[0].wait()

    for i, k in enumerate(STEPS):
        q = lax.rem(r + k, reps)

        def pack(j, carry, i=i, q=q):
            block = tab[ROW_BLOCK, CAP * j + q]
            for c in range(CHUNKS):
                rs_send[c, i, j] = grad[block, :, cols[c]]
            return carry

        lax.fori_loop(0, places, pack, 0)

    pl.semaphore_wait(barrier, reps - 1 + devs - 1)

    def over_rep(src, dst, ss, rs):
        copies = []
        for i, k in enumerate(STEPS):
            copies.append(
                pltpu.make_async_remote_copy(
                    src_ref=src(i),
                    dst_ref=dst(i),
                    send_sem=ss.at[i],
                    recv_sem=rs.at[i],
                    device_id=rep_peer(k),
                    device_id_type=MESH,
                )
            )
        for copy in copies:
            copy.start()
        return copies

    rs = [
        over_rep(lambda i: rs_send.at[c, i], lambda i: rs_recv.at[c, i], rs_ss.at[c], rs_rs.at[c])
        for c in range(CHUNKS)
    ]

    def one(src, dst, ss, rs, to):
        pltpu.make_async_remote_copy(
            src_ref=src, dst_ref=dst, send_sem=ss, recv_sem=rs, device_id=(r, to), device_id_type=MESH
        ).start()

    ag = []
    for c in range(CHUNKS):
        for copy in rs[c]:
            copy.wait_recv()

        def add(j, carry, c=c):
            block = tab[ROW_BLOCK, CAP * j + r]
            total = grad[block, :, cols[c]].astype(jnp.float32)
            for i in range(len(STEPS)):
                total += rs_recv[c, i, j].astype(jnp.float32)
            s_own[c][j] = total.astype(jnp.bfloat16)
            return carry

        lax.fori_loop(0, places, add, 0)

        def to_owner(t, carry, c=c):
            o = dp_peer(t)
            stage[0, o, :, cols[c]] = s_own[c][tab[ROW_PLACE + r, o]]
            one(stage.at[0, o, :, cols[c]], gath.at[0, mine, cols[c]], pr_ss.at[c], pr_rs.at[c], o)
            return carry

        lax.fori_loop(1, devs, to_owner, 0)
        gath[0, mine, cols[c]] = s_own[c][tab[ROW_PLACE + r, d]]
        ag.append(over_rep(lambda i: s_own[c], lambda i: s_recv[i].at[c], ag_ss.at[c], ag_rs.at[c]))

    slot = (r - tab[ROW_START, d]) & 3
    loads[1].wait()
    loads[2].wait()
    for c in range(CHUNKS):
        arrived = gath.at[0, pl.ds(0, rows * (devs - 1)), cols[c]]
        pltpu.make_async_copy(arrived, arrived, pr_rs.at[c]).wait()
        for m in range(0, width, tile):
            half[m : m + tile, cols[c]] = jnp.dot(
                lroot[slot, m : m + tile, :], gath[0, :, cols[c]], preferred_element_type=jnp.float32
            ).astype(jnp.bfloat16)
    grad_sq = jnp.zeros((1, 1), jnp.float32)
    dir_sq = jnp.zeros((1, 1), jnp.float32)
    for m in range(0, width, tile):
        piece = jnp.dot(half[m : m + tile, :], rroot[slot], preferred_element_type=jnp.float32)
        direct[m : m + tile, :] = piece
        dir_sq += jnp.sum(piece * piece, keepdims=True)
        g = gath[0, m : m + tile, :].astype(jnp.float32)
        grad_sq += jnp.sum(g * g, keepdims=True)
    scale = jnp.sqrt(grad_sq) / jnp.sqrt(dir_sq + EPS)
    for m in range(0, width, tile):
        upd[m : m + tile, :] = (direct[m : m + tile, :] * scale).astype(jnp.bfloat16)

    for c in range(CHUNKS):

        def homeward(t, carry, c=c):
            to = dp_peer(t)
            theirs = pl.ds(pl.multiple_of(to * rows, rows), rows)
            one(upd.at[theirs, cols[c]], back[c].at[d], bk_ss.at[c], bk_rs.at[c], to)
            return carry

        lax.fori_loop(1, devs, homeward, 0)
        back[c][d] = upd[mine, cols[c]]

    for i, k in enumerate(STEPS):
        for c in range(CHUNKS):
            ag[c][i].wait_recv()
        q = lax.rem(r + reps - k, reps)

        def to_owner_too(t, carry, i=i, q=q):
            o = dp_peer(t)
            place = tab[ROW_PLACE + q, o]
            for c in range(CHUNKS):
                stage[1 + i, o, :, cols[c]] = s_recv[i][c, place]
            one(stage.at[1 + i, o], gath.at[1 + i, mine, :], ot_ss.at[i], ot_rs.at[i], o)
            return carry

        lax.fori_loop(1, devs, to_owner_too, 0)
        own = tab[ROW_PLACE + q, d]
        for c in range(CHUNKS):
            gath[1 + i, mine, cols[c]] = s_recv[i][c, own]

    au = []
    for c in range(CHUNKS):
        arrived = back[c].at[pl.ds(0, devs - 1)]
        pltpu.make_async_copy(arrived, arrived, bk_rs.at[c]).wait()

        def unpack(j, carry, c=c):
            uall[0, j, :, cols[c]] = back[c][tab[ROW_OWNER, CAP * j + r]]
            return carry

        lax.fori_loop(0, places, unpack, 0)
        au.append(
            over_rep(
                lambda i: uall.at[0, :, :, cols[c]],
                lambda i: uall.at[1 + i, :, :, cols[c]],
                au_ss.at[c],
                au_rs.at[c],
            )
        )

    for c in range(CHUNKS):
        for copy in rs[c] + ag[c]:
            copy.wait_send()
        sent = stage.at[0, pl.ds(0, devs - 1), :, cols[c]]
        pltpu.make_async_copy(sent, sent, pr_ss.at[c]).wait()
        sent = back[c].at[pl.ds(0, devs - 1)]
        pltpu.make_async_copy(sent, sent, bk_ss.at[c]).wait()
    for i in range(len(STEPS)):
        sent = stage.at[1 + i, pl.ds(0, devs - 1)]
        pltpu.make_async_copy(sent, sent, ot_ss.at[i]).wait()
        arrived = gath.at[1 + i, pl.ds(0, rows * (devs - 1)), :]
        pltpu.make_async_copy(arrived, arrived, ot_rs.at[i]).wait()
    for copies in au:
        for copy in copies:
            copy.wait()
    loads[3].wait()
    loads[4].wait()


def write_out(
    reps, tab_v, gath, uall, lf, rf, update, left_out, right_out, tab, left_buf, right_buf, sems
):
    r = lax.axis_index("rep")
    d = lax.axis_index("dp")
    blocks, width = update.shape[0], gath.shape[2]
    places = uall.shape[1]
    tile = min(256, width)
    load = pltpu.make_async_copy(tab_v, tab, sems.at[0])
    load.start()
    load.wait()

    def buffer_of(q):
        step = lax.rem(r - q + reps, reps)
        return jnp.where(step < 2, step, 5 - step)

    def put(b, carry):
        pos = tab[ROW_POS, b]
        pltpu.make_async_copy(uall.at[buffer_of(pos & 3), pos >> 2], update.at[b], sems.at[1]).start()
        return carry

    lax.fori_loop(0, blocks, put, 0)
    start, count = tab[ROW_START, d], tab[ROW_COUNT, d]
    weight = (1.0 - DECAY) / width
    copies = []
    for s in range(CAP):
        valid = s < count
        idx = buffer_of((start + s) & 3)
        for side, (factor, buf, out) in enumerate(((lf, left_buf, left_out), (rf, right_buf, right_out))):
            for m in range(0, width, tile):
                sl = pl.ds(m, tile)
                if side == 0:
                    gram = lax.dot_general(
                        gath[idx, sl, :], gath[idx], (((1,), (1,)), ((), ())), preferred_element_type=jnp.float32
                    )
                else:
                    gram = lax.dot_general(
                        gath[idx, :, sl], gath[idx], (((0,), (0,)), ((), ())), preferred_element_type=jnp.float32
                    )
                buf[s, sl, :] = DECAY * factor[s, sl, :] + jnp.where(valid, weight * gram, 0.0)
                copy = pltpu.make_async_copy(buf.at[s, sl], out.at[s, sl], sems.at[2])
                copy.start()
                copies.append(copy)
    pltpu.make_async_copy(left_buf, left_out, sems.at[2]).wait()
    pltpu.make_async_copy(right_buf, right_out, sems.at[2]).wait()
    flat = uall
    pltpu.make_async_copy(flat, flat, sems.at[1]).wait()


def shards(reps, devs, gradient, owner, left_factor, right_factor, left_root, right_root):
    bf16, f32 = jnp.bfloat16, jnp.float32
    _, blocks, rows, width = gradient.shape
    places = blocks // reps
    part = width // CHUNKS
    any_spec = pl.BlockSpec(memory_space=pl.ANY)
    vmem_spec = pl.BlockSpec(memory_space=pltpu.VMEM)
    dma = pltpu.SemaphoreType.DMA
    three = len(STEPS)
    tab, gath, uall, lf, rf = pl.pallas_call(
        functools.partial(exchange, reps, devs),
        name="exchange",
        out_shape=[
            in_vmem((TAB_ROWS, 128), jnp.int32),
            in_vmem((CAP, width, width), bf16),
            in_vmem((CAP, places, rows, width), bf16),
            in_vmem((CAP, width, width), f32),
            in_vmem((CAP, width, width), f32),
        ],
        in_specs=[vmem_spec] + [any_spec] * 5,
        out_specs=[vmem_spec] * 5,
        scratch_shapes=[
            pltpu.SMEM((TAB_ROWS, 128), jnp.int32),
            pltpu.VMEM((blocks, rows, width), bf16),
            pltpu.VMEM((CAP, width, width), bf16),
            pltpu.VMEM((CAP, width, width), bf16),
            pltpu.VMEM((CHUNKS, three, places, rows, part), bf16),
            pltpu.VMEM((CHUNKS, three, places, rows, part), bf16),
            pltpu.VMEM((CAP, devs, rows, width), bf16),
            pltpu.VMEM((width, width), bf16),
            pltpu.VMEM((width, width), f32),
            pltpu.VMEM((width, width), bf16),
            [pltpu.VMEM((places, rows, part), bf16)] * CHUNKS,
            [pltpu.VMEM((CHUNKS, places, rows, part), bf16)] * three,
            [pltpu.VMEM((devs, rows, part), bf16)] * CHUNKS,
            dma((6,)),
            dma((CHUNKS, three)),
            dma((CHUNKS, three)),
            dma((CHUNKS, three)),
            dma((CHUNKS, three)),
            dma((CHUNKS,)),
            dma((CHUNKS,)),
            dma((three,)),
            dma((three,)),
            dma((CHUNKS,)),
            dma((CHUNKS,)),
            dma((CHUNKS, three)),
            dma((CHUNKS, three)),
        ],
        compiler_params=pltpu.CompilerParams(
            collective_id=0, has_side_effects=True, vmem_limit_bytes=40 * 2**20
        ),
    )(owner.reshape(1, blocks), gradient[0], left_factor, right_factor, left_root, right_root)
    update, left_out, right_out = pl.pallas_call(
        functools.partial(write_out, reps),
        name="write_out",
        out_shape=[
            jax.ShapeDtypeStruct((blocks, rows, width), bf16),
            jax.ShapeDtypeStruct((CAP, width, width), f32),
            jax.ShapeDtypeStruct((CAP, width, width), f32),
        ],
        in_specs=[any_spec] + [vmem_spec] * 4,
        out_specs=[pl.BlockSpec(memory_space=pltpu.HBM)] * 3,
        scratch_shapes=[
            pltpu.SMEM((TAB_ROWS, 128), jnp.int32),
            pltpu.VMEM((CAP, width, width), f32),
            pltpu.VMEM((CAP, width, width), f32),
            dma((3,)),
        ],
        compiler_params=pltpu.CompilerParams(vmem_limit_bytes=24 * 2**20),
    )(tab, *(from_vmem(x) for x in (gath, uall, lf, rf)))
    return update, left_out, right_out


def solution(mesh):
    in_specs = (
        P("rep", None, "dp", None),
        P(),
        P("dp", None, None),
        P("dp", None, None),
        P("dp", None, None),
        P("dp", None, None),
    )
    out_specs = (P(None, "dp", None), P("dp", None, None), P("dp", None, None))
    body = functools.partial(shards, mesh.shape["rep"], mesh.shape["dp"])
    return jax.shard_map(body, mesh=mesh, in_specs=in_specs, out_specs=out_specs, check_vma=False)
```

```python
import functools

import jax
import jax.numpy as jnp
from jax import lax
from jax.experimental import pallas as pl
from jax.experimental.pallas import tpu as pltpu
from jax.sharding import PartitionSpec as P

MESH = pl.DeviceIdType.MESH
CAP = 4
DECAY = 0.9
EPS = 1e-06
CHUNKS = 2
PIECES = 6
STEPS = (1, 3, 2)
TAB_ROWS = 16
ROW_BLOCK, ROW_POS, ROW_OWNER, ROW_START, ROW_COUNT, ROW_PLACE = 0, 1, 2, 3, 4, 5


def in_vmem(shape, dtype):
    return pltpu.VMEM(shape, dtype)


def from_vmem(x):
    return pltpu.with_memory_space_constraint(x, pltpu.VMEM)


def fill_tables(owner_ref, tab_ref):
    blocks = owner_ref.shape[1]
    lanes = tab_ref.shape[1]
    b = lax.broadcasted_iota(jnp.int32, (blocks, lanes), 0)
    c = lax.broadcasted_iota(jnp.int32, (blocks, lanes), 1)

    def down(x):
        return jnp.sum(x, axis=0, keepdims=True)

    inside = c < blocks
    row = jnp.broadcast_to(jnp.pad(owner_ref[...], ((0, 0), (0, lanes - blocks))), (blocks, lanes))
    col = jnp.sum(jnp.where(b == c, row, 0), axis=1, keepdims=True)
    col = jnp.broadcast_to(col, (blocks, lanes))
    before = (row < col) | ((row == col) & (c < b))
    pos_col = jnp.sum(jnp.where(before & inside, 1, 0), axis=1, keepdims=True)
    pos_col = jnp.broadcast_to(pos_col, (blocks, lanes))
    after = (col < row) | ((col == row) & (b < c))
    pos_row = down(jnp.where(after, 1, 0))
    here = pos_col == c
    start = down(jnp.where(col < c, 1, 0))
    count = down(jnp.where(col == c, 1, 0))
    tab_ref[ROW_BLOCK : ROW_BLOCK + 1, :] = down(jnp.where(here, b, 0))
    tab_ref[ROW_POS : ROW_POS + 1, :] = pos_row
    tab_ref[ROW_OWNER : ROW_OWNER + 1, :] = down(jnp.where(here, col, 0))
    tab_ref[ROW_START : ROW_START + 1, :] = start
    tab_ref[ROW_COUNT : ROW_COUNT + 1, :] = count
    for q in range(CAP):
        slot = (q - start) & 3
        place = jnp.where(slot < count, (start + slot) >> 2, 0)
        tab_ref[ROW_PLACE + q : ROW_PLACE + q + 1, :] = place
    rest = ROW_PLACE + CAP
    tab_ref[rest:, :] = jnp.zeros((TAB_ROWS - rest, lanes), jnp.int32)


def exchange(
    reps, devs, owner_hbm, grad_hbm, lf_hbm, rf_hbm, lr_hbm, rr_hbm,
    tab_out, gath, uall, lf_out, rf_out,
    tab, owner, grad, lroot, rroot, rs_send, rs_recv, stage, half, direct, upd, s_own, s_recv, back,
    loc_sem, rs_ss, rs_rs, ag_ss, ag_rs, pr_ss, pr_rs, ot_ss, ot_rs, bk_ss, bk_rs, au_ss, au_rs,
):
    r = lax.axis_index("rep")
    d = lax.axis_index("dp")
    places, rows, width = s_own[0].shape[0], grad.shape[1], grad.shape[2]
    part = width // CHUNKS
    cols = [pl.ds(c * part, part) for c in range(CHUNKS)]
    tile = min(256, width)
    mine = pl.ds(pl.multiple_of(d * rows, rows), rows)
    few = places // 2
    first, last = pl.ds(0, few), pl.ds(few, few)

    def rep_of(k):
        return lax.rem(r + k, reps)

    def dp_peer(t):
        return lax.rem(d + t, devs)

    def local(src, dst, i):
        return pltpu.make_async_copy(src, dst, loc_sem.at[i])

    load_owner, load_grad = local(owner_hbm, owner, 0), local(grad_hbm, grad, 1)
    load_roots = [local(lr_hbm, lroot, 2), local(rr_hbm, rroot, 3)]
    load_factors = [local(lf_hbm, lf_out, 4), local(rf_hbm, rf_out, 5)]
    load_owner.start()
    load_grad.start()

    barrier = pltpu.get_barrier_semaphore()
    for k in STEPS:
        pl.semaphore_signal(barrier, inc=1, device_id=(rep_of(k), d), device_id_type=MESH)

    def greet(t, carry):
        pl.semaphore_signal(barrier, inc=1, device_id=(r, dp_peer(t)), device_id_type=MESH)
        return carry

    lax.fori_loop(1, devs, greet, 0)

    load_owner.wait()
    fill_tables(owner, tab_out)
    to_scalars = local(tab_out, tab, 6)
    to_scalars.start()
    to_scalars.wait()
    load_grad.wait()

    def to_rep(piece, src, dst, ss, rs):
        copy = pltpu.make_async_remote_copy(
            src_ref=src,
            dst_ref=dst,
            send_sem=ss.at[piece],
            recv_sem=rs.at[piece],
            device_id=(rep_of(1 if piece % 2 == 0 else reps - 1), d),
            device_id_type=MESH,
        )
        copy.start()
        return copy

    packing = ((2, 0), (2, few), (1, few), (reps - 1, 0), (1, 0), (reps - 1, few))

    def pack(pieces, c):
        def step(j, carry):
            for p in pieces:
                k, at = packing[p]
                block = tab[ROW_BLOCK, CAP * (at + j) + rep_of(k)]
                rows_here = grad[block, :, cols[c]]
                if p >= 4:
                    both = rows_here.astype(jnp.float32) + rs_recv[c, p - 4, j].astype(jnp.float32)
                    rows_here = both.astype(jnp.bfloat16)
                rs_send[c, p, j] = rows_here
            return carry

        lax.fori_loop(0, few, step, 0)

    def send_sums(p, c):
        return to_rep(p, rs_send.at[c, p], rs_recv.at[c, p], rs_ss.at[c], rs_rs.at[c])

    for c in range(CHUNKS):
        pack((0, 1, 2, 3), c)
    pl.semaphore_wait(barrier, reps - 1 + devs - 1)
    rs = [[send_sums(p, c) for p in range(4)] for c in range(CHUNKS)]
    for load in load_roots + load_factors:
        load.start()
    for c in range(CHUNKS):
        for p in (4, 5):
            rs[c][p - 4].wait_recv()
            pack((p,), c)
            rs[c].append(send_sums(p, c))

    def share(buf, ss, rs):
        return [
            to_rep(0, buf(0, first), buf(1, first), ss, rs),
            to_rep(1, buf(0, last), buf(2, last), ss, rs),
            to_rep(2, buf(0, last), buf(1, last), ss, rs),
            to_rep(3, buf(0, first), buf(2, first), ss, rs),
        ]

    def pass_on(copies, buf, ss, rs):
        copies[0].wait_recv()
        copies.append(to_rep(4, buf(1, first), buf(3, first), ss, rs))
        copies[1].wait_recv()
        copies.append(to_rep(5, buf(2, last), buf(3, last), ss, rs))

    def sums(c):
        return lambda i, sl: (s_own[c] if i == 0 else s_recv[(i - 1) * CHUNKS + c]).at[sl]

    def one(src, dst, ss, rs, to):
        pltpu.make_async_remote_copy(
            src_ref=src, dst_ref=dst, send_sem=ss, recv_sem=rs, device_id=(r, to), device_id_type=MESH
        ).start()

    def to_owners(i, c, q, src, ss, rs):
        def step(t, carry):
            o = dp_peer(t)
            stage[i, o, :, cols[c]] = src[tab[ROW_PLACE + q, o]]
            one(stage.at[i, o, :, cols[c]], gath.at[i, mine, cols[c]], ss, rs, o)
            return carry

        lax.fori_loop(1, devs, step, 0)
        gath[i, mine, cols[c]] = src[tab[ROW_PLACE + q, d]]

    ag = []
    for c in range(CHUNKS):
        for p in (2, 3, 4, 5):
            rs[c][p].wait_recv()

        def add(j, carry, c=c):
            for at, pieces in ((0, (4, 3)), (few, (2, 5))):
                total = grad[tab[ROW_BLOCK, CAP * (at + j) + r], :, cols[c]].astype(jnp.float32)
                for p in pieces:
                    total += rs_recv[c, p, j].astype(jnp.float32)
                s_own[c][at + j] = total.astype(jnp.bfloat16)
            return carry

        lax.fori_loop(0, few, add, 0)
        ag.append(share(sums(c), ag_ss.at[c], ag_rs.at[c]))
        to_owners(0, c, r, s_own[c], pr_ss.at[c], pr_rs.at[c])

    def pass_sums_on(c):
        pass_on(ag[c], sums(c), ag_ss.at[c], ag_rs.at[c])

    def others(i, c):
        for p in ((2,), (3,), (4, 5))[i - 1]:
            ag[c][p].wait_recv()
        q = rep_of(reps - STEPS[i - 1])
        to_owners(i, c, q, s_recv[(i - 1) * CHUNKS + c], ot_ss.at[c, i - 1], ot_rs.at[c, i - 1])

    pass_sums_on(0)
    others(1, 0)
    others(2, 0)
    for c in range(1, CHUNKS):
        pass_sums_on(c)

    slot = (r - tab[ROW_START, d]) & 3
    for load in load_roots:
        load.wait()
    for c in range(CHUNKS):
        arrived = gath.at[0, pl.ds(0, rows * (devs - 1)), cols[c]]
        pltpu.make_async_copy(arrived, arrived, pr_rs.at[c]).wait()
        for m in range(0, width, tile):
            half[m : m + tile, cols[c]] = jnp.dot(
                lroot[slot, m : m + tile, :], gath[0, :, cols[c]], preferred_element_type=jnp.float32
            ).astype(jnp.bfloat16)
    grad_sq = jnp.zeros((1, 1), jnp.float32)
    dir_sq = jnp.zeros((1, 1), jnp.float32)
    for m in range(0, width, tile):
        piece = jnp.dot(half[m : m + tile, :], rroot[slot], preferred_element_type=jnp.float32)
        direct[m : m + tile, :] = piece
        dir_sq += jnp.sum(piece * piece, keepdims=True)
        g = gath[0, m : m + tile, :].astype(jnp.float32)
        grad_sq += jnp.sum(g * g, keepdims=True)
    scale = jnp.sqrt(grad_sq) / jnp.sqrt(dir_sq + EPS)
    for m in range(0, width, tile):
        upd[m : m + tile, :] = (direct[m : m + tile, :] * scale).astype(jnp.bfloat16)

    for c in range(CHUNKS):

        def homeward(t, carry, c=c):
            to = dp_peer(t)
            theirs = pl.ds(pl.multiple_of(to * rows, rows), rows)
            one(upd.at[theirs, cols[c]], back[c].at[d], bk_ss.at[c], bk_rs.at[c], to)
            return carry

        lax.fori_loop(1, devs, homeward, 0)
        back[c][d] = upd[mine, cols[c]]

    others(3, 0)
    for c in range(1, CHUNKS):
        for i in (1, 2, 3):
            others(i, c)

    def steps(c):
        return lambda i, sl: uall.at[i, sl, :, cols[c]]

    au = []
    for c in range(CHUNKS):
        arrived = back[c].at[pl.ds(0, devs - 1)]
        pltpu.make_async_copy(arrived, arrived, bk_rs.at[c]).wait()

        def unpack(j, carry, c=c):
            uall[0, j, :, cols[c]] = back[c][tab[ROW_OWNER, CAP * j + r]]
            return carry

        lax.fori_loop(0, places, unpack, 0)
        au.append(share(steps(c), au_ss.at[c], au_rs.at[c]))
    for c in range(CHUNKS):
        pass_on(au[c], steps(c), au_ss.at[c], au_rs.at[c])

    for c in range(CHUNKS):
        for copy in rs[c] + ag[c] + au[c]:
            copy.wait_send()
        for i in range(CAP):
            sent = stage.at[i, pl.ds(0, devs - 1), :, cols[c]]
            pltpu.make_async_copy(sent, sent, pr_ss.at[c] if i == 0 else ot_ss.at[c, i - 1]).wait()
        for i in range(1, CAP):
            arrived = gath.at[i, pl.ds(0, rows * (devs - 1)), cols[c]]
            pltpu.make_async_copy(arrived, arrived, ot_rs.at[c, i - 1]).wait()
        sent = back[c].at[pl.ds(0, devs - 1)]
        pltpu.make_async_copy(sent, sent, bk_ss.at[c]).wait()
        for copy in au[c][2:]:
            copy.wait_recv()
    for load in load_factors:
        load.wait()


def write_out(
    reps, tab_v, gath, uall, lf, rf, update, left_out, right_out, tab, left_buf, right_buf, sems
):
    r = lax.axis_index("rep")
    d = lax.axis_index("dp")
    blocks, width = update.shape[0], gath.shape[2]
    places = uall.shape[1]
    tile = min(256, width)
    load = pltpu.make_async_copy(tab_v, tab, sems.at[0])
    load.start()
    load.wait()

    def buffer_of(q):
        step = lax.rem(r - q + reps, reps)
        return jnp.where(step < 2, step, 5 - step)

    def put(b, carry):
        pos = tab[ROW_POS, b]
        pltpu.make_async_copy(uall.at[buffer_of(pos & 3), pos >> 2], update.at[b], sems.at[1]).start()
        return carry

    lax.fori_loop(0, blocks, put, 0)
    start, count = tab[ROW_START, d], tab[ROW_COUNT, d]
    weight = (1.0 - DECAY) / width
    copies = []
    for s in range(CAP):
        valid = s < count
        idx = buffer_of((start + s) & 3)
        for side, (factor, buf, out) in enumerate(((lf, left_buf, left_out), (rf, right_buf, right_out))):
            for m in range(0, width, tile):
                sl = pl.ds(m, tile)
                if side == 0:
                    gram = lax.dot_general(
                        gath[idx, sl, :], gath[idx], (((1,), (1,)), ((), ())), preferred_element_type=jnp.float32
                    )
                else:
                    gram = lax.dot_general(
                        gath[idx, :, sl], gath[idx], (((0,), (0,)), ((), ())), preferred_element_type=jnp.float32
                    )
                buf[s, sl, :] = DECAY * factor[s, sl, :] + jnp.where(valid, weight * gram, 0.0)
                copy = pltpu.make_async_copy(buf.at[s, sl], out.at[s, sl], sems.at[2])
                copy.start()
                copies.append(copy)
    pltpu.make_async_copy(left_buf, left_out, sems.at[2]).wait()
    pltpu.make_async_copy(right_buf, right_out, sems.at[2]).wait()
    flat = uall
    pltpu.make_async_copy(flat, flat, sems.at[1]).wait()


def shards(reps, devs, gradient, owner, left_factor, right_factor, left_root, right_root):
    bf16, f32 = jnp.bfloat16, jnp.float32
    _, blocks, rows, width = gradient.shape
    places = blocks // reps
    part = width // CHUNKS
    any_spec = pl.BlockSpec(memory_space=pl.ANY)
    hbm_spec = pl.BlockSpec(memory_space=pltpu.HBM)
    vmem_spec = pl.BlockSpec(memory_space=pltpu.VMEM)
    dma = pltpu.SemaphoreType.DMA
    three = len(STEPS)
    tab, gath, uall, lf, rf = pl.pallas_call(
        functools.partial(exchange, reps, devs),
        name="exchange",
        out_shape=[
            in_vmem((TAB_ROWS, 128), jnp.int32),
            in_vmem((CAP, width, width), bf16),
            in_vmem((CAP, places, rows, width), bf16),
            in_vmem((CAP, width, width), f32),
            in_vmem((CAP, width, width), f32),
        ],
        in_specs=[hbm_spec] * 6,
        out_specs=[vmem_spec] * 5,
        scratch_shapes=[
            pltpu.SMEM((TAB_ROWS, 128), jnp.int32),
            pltpu.VMEM((1, blocks), jnp.int32),
            pltpu.VMEM((blocks, rows, width), bf16),
            pltpu.VMEM((CAP, width, width), bf16),
            pltpu.VMEM((CAP, width, width), bf16),
            pltpu.VMEM((CHUNKS, PIECES, places // 2, rows, part), bf16),
            pltpu.VMEM((CHUNKS, PIECES, places // 2, rows, part), bf16),
            pltpu.VMEM((CAP, devs, rows, width), bf16),
            pltpu.VMEM((width, width), bf16),
            pltpu.VMEM((width, width), f32),
            pltpu.VMEM((width, width), bf16),
            [pltpu.VMEM((places, rows, part), bf16)] * CHUNKS,
            [pltpu.VMEM((places, rows, part), bf16)] * (CHUNKS * three),
            [pltpu.VMEM((devs, rows, part), bf16)] * CHUNKS,
            dma((7,)),
            dma((CHUNKS, PIECES)),
            dma((CHUNKS, PIECES)),
            dma((CHUNKS, PIECES)),
            dma((CHUNKS, PIECES)),
            dma((CHUNKS,)),
            dma((CHUNKS,)),
            dma((CHUNKS, three)),
            dma((CHUNKS, three)),
            dma((CHUNKS,)),
            dma((CHUNKS,)),
            dma((CHUNKS, PIECES)),
            dma((CHUNKS, PIECES)),
        ],
        compiler_params=pltpu.CompilerParams(
            collective_id=0, has_side_effects=True, vmem_limit_bytes=40 * 2**20
        ),
    )(owner.reshape(1, blocks), gradient[0], left_factor, right_factor, left_root, right_root)
    update, left_out, right_out = pl.pallas_call(
        functools.partial(write_out, reps),
        name="write_out",
        out_shape=[
            jax.ShapeDtypeStruct((blocks, rows, width), bf16),
            jax.ShapeDtypeStruct((CAP, width, width), f32),
            jax.ShapeDtypeStruct((CAP, width, width), f32),
        ],
        in_specs=[any_spec] + [vmem_spec] * 4,
        out_specs=[hbm_spec] * 3,
        scratch_shapes=[
            pltpu.SMEM((TAB_ROWS, 128), jnp.int32),
            pltpu.VMEM((CAP, width, width), f32),
            pltpu.VMEM((CAP, width, width), f32),
            dma((3,)),
        ],
        compiler_params=pltpu.CompilerParams(vmem_limit_bytes=24 * 2**20),
    )(tab, *(from_vmem(x) for x in (gath, uall, lf, rf)))
    return update, left_out, right_out


def solution(mesh):
    in_specs = (
        P("rep", None, "dp", None),
        P(),
        P("dp", None, None),
        P("dp", None, None),
        P("dp", None, None),
        P("dp", None, None),
    )
    out_specs = (P(None, "dp", None), P("dp", None, None), P("dp", None, None))
    body = functools.partial(shards, mesh.shape["rep"], mesh.shape["dp"])
    return jax.shard_map(body, mesh=mesh, in_specs=in_specs, out_specs=out_specs, check_vma=False)
```

```python
import functools

import jax
import jax.numpy as jnp
from jax import lax
from jax.experimental import pallas as pl
from jax.experimental.pallas import tpu as pltpu
from jax.sharding import PartitionSpec as P

MESH = pl.DeviceIdType.MESH
CAP = 4
DECAY = 0.9
EPS = 1e-06
CHUNKS = 2
PIECES = 6
STEPS = (1, 3, 2)
TAB_ROWS = 16
ROW_BLOCK, ROW_POS, ROW_OWNER, ROW_START, ROW_COUNT, ROW_PLACE = 0, 1, 2, 3, 4, 5


def far_order():
    near = {0: 0, 1: 1, 2: 2, 3: 1}
    every = [(z, x, c) for z in range(4) for x in range(4) for c in range(2) if (z, x, c) != (0, 0, 0)]
    return sorted(every, key=lambda p: -(near[p[0]] + near[p[1]]))


def in_vmem(shape, dtype):
    return pltpu.VMEM(shape, dtype)


def in_hbm(x):
    return pltpu.with_memory_space_constraint(x, pltpu.HBM)


def from_vmem(x):
    return pltpu.with_memory_space_constraint(x, pltpu.VMEM)


def fill_tables(owner_ref, tab_ref):
    blocks = owner_ref.shape[1]
    lanes = tab_ref.shape[1]
    b = lax.broadcasted_iota(jnp.int32, (blocks, lanes), 0)
    c = lax.broadcasted_iota(jnp.int32, (blocks, lanes), 1)

    def down(x):
        return jnp.sum(x, axis=0, keepdims=True)

    inside = c < blocks
    row = jnp.broadcast_to(jnp.pad(owner_ref[...], ((0, 0), (0, lanes - blocks))), (blocks, lanes))
    col = jnp.sum(jnp.where(b == c, row, 0), axis=1, keepdims=True)
    col = jnp.broadcast_to(col, (blocks, lanes))
    before = (row < col) | ((row == col) & (c < b))
    pos_col = jnp.sum(jnp.where(before & inside, 1, 0), axis=1, keepdims=True)
    pos_col = jnp.broadcast_to(pos_col, (blocks, lanes))
    after = (col < row) | ((col == row) & (b < c))
    pos_row = down(jnp.where(after, 1, 0))
    here = pos_col == c
    start = down(jnp.where(col < c, 1, 0))
    count = down(jnp.where(col == c, 1, 0))
    tab_ref[ROW_BLOCK : ROW_BLOCK + 1, :] = down(jnp.where(here, b, 0))
    tab_ref[ROW_POS : ROW_POS + 1, :] = pos_row
    tab_ref[ROW_OWNER : ROW_OWNER + 1, :] = down(jnp.where(here, col, 0))
    tab_ref[ROW_START : ROW_START + 1, :] = start
    tab_ref[ROW_COUNT : ROW_COUNT + 1, :] = count
    for q in range(CAP):
        slot = (q - start) & 3
        place = jnp.where(slot < count, (start + slot) >> 2, 0)
        tab_ref[ROW_PLACE + q : ROW_PLACE + q + 1, :] = place
    rest = ROW_PLACE + CAP
    tab_ref[rest:, :] = jnp.zeros((TAB_ROWS - rest, lanes), jnp.int32)


def exchange(
    reps, devs, owner_hbm, grad_hbm, lf_hbm, rf_hbm, lr_hbm, rr_hbm,
    tab_out, left_gram, right_gram, uall, lf_out, rf_out,
    tab, gath, owner, grad, lroot, rroot, rs_send, rs_recv, stage, half, direct, upd, s_own, s_recv, back,
    loc_sem, rs_ss, rs_rs, ag_ss, ag_rs, pr_ss, pr_rs, ot_ss, ot_rs, ow_ss, ow_rs, bk_ss, bk_rs, au_ss, au_rs,
):
    r = lax.axis_index("rep")
    d = lax.axis_index("dp")
    places, rows, width = s_own[0].shape[0], grad.shape[1], grad.shape[2]
    part = width // CHUNKS
    cols = [pl.ds(c * part, part) for c in range(CHUNKS)]
    tile = min(256, width)
    mine = pl.ds(pl.multiple_of(d * rows, rows), rows)
    few = places // 2
    first, last = pl.ds(0, few), pl.ds(few, few)

    def rep_of(k):
        return lax.rem(r + k, reps)

    def dp_peer(t):
        if not isinstance(t, tuple):
            return lax.rem(d + t, devs)
        dz, dx, dc = t
        z, x, c = d // 8, lax.rem(d // 2, 4), lax.rem(d, 2)
        return lax.rem(z + dz, 4) * 8 + lax.rem(x + dx, 4) * 2 + lax.rem(c + dc, 2)

    def local(src, dst, i):
        return pltpu.make_async_copy(src, dst, loc_sem.at[i])

    load_owner, load_grad = local(owner_hbm, owner, 0), local(grad_hbm.at[0], grad, 1)
    load_roots = [local(lr_hbm, lroot, 2), local(rr_hbm, rroot, 3)]
    load_factors = [local(lf_hbm, lf_out, 4), local(rf_hbm, rf_out, 5)]
    load_owner.start()
    load_grad.start()

    barrier = pltpu.get_barrier_semaphore()
    for k in STEPS:
        pl.semaphore_signal(barrier, inc=1, device_id=(rep_of(k), d), device_id_type=MESH)

    def greet(t, carry):
        pl.semaphore_signal(barrier, inc=1, device_id=(r, dp_peer(t)), device_id_type=MESH)
        return carry

    lax.fori_loop(1, devs, greet, 0)

    load_owner.wait()
    fill_tables(owner, tab_out)
    to_scalars = local(tab_out, tab, 6)
    to_scalars.start()
    to_scalars.wait()
    load_grad.wait()

    def to_rep(piece, src, dst, ss, rs):
        copy = pltpu.make_async_remote_copy(
            src_ref=src,
            dst_ref=dst,
            send_sem=ss.at[piece],
            recv_sem=rs.at[piece],
            device_id=(rep_of(1 if piece % 2 == 0 else reps - 1), d),
            device_id_type=MESH,
        )
        copy.start()
        return copy

    packing = ((2, 0), (2, few), (1, few), (reps - 1, 0), (1, 0), (reps - 1, few))

    def pack(pieces, c):
        def step(j, carry):
            for p in pieces:
                k, at = packing[p]
                block = tab[ROW_BLOCK, CAP * (at + j) + rep_of(k)]
                rows_here = grad[block, :, cols[c]]
                if p >= 4:
                    both = rows_here.astype(jnp.float32) + rs_recv[c, p - 4, j].astype(jnp.float32)
                    rows_here = both.astype(jnp.bfloat16)
                rs_send[c, p, j] = rows_here
            return carry

        lax.fori_loop(0, few, step, 0)

    def send_sums(p, c):
        return to_rep(p, rs_send.at[c, p], rs_recv.at[c, p], rs_ss.at[c], rs_rs.at[c])

    for c in range(CHUNKS):
        pack((0, 1, 2, 3), c)
    pl.semaphore_wait(barrier, reps - 1 + devs - 1)
    rs = [[send_sums(p, c) for p in range(4)] for c in range(CHUNKS)]
    for load in load_roots + load_factors:
        load.start()
    for c in range(CHUNKS):
        for p in (4, 5):
            rs[c][p - 4].wait_recv()
            pack((p,), c)
            rs[c].append(send_sums(p, c))

    def share(pieces, buf, ss, rs):
        halves = (first, last, last, first)
        return {p: to_rep(p, buf(0, halves[p]), buf(1 + p % 2, halves[p]), ss, rs) for p in pieces}

    def pass_on(copies, buf, ss, rs):
        copies[0].wait_recv()
        copies[4] = to_rep(4, buf(1, first), buf(3, first), ss, rs)
        copies[1].wait_recv()
        copies[5] = to_rep(5, buf(2, last), buf(3, last), ss, rs)

    def sums(c):
        return lambda i, sl: (s_own[c] if i == 0 else s_recv[(i - 1) * CHUNKS + c]).at[sl]

    def one(src, dst, ss, rs, to):
        pltpu.make_async_remote_copy(
            src_ref=src, dst_ref=dst, send_sem=ss, recv_sem=rs, device_id=(r, to), device_id_type=MESH
        ).start()

    def to_owners(i, c, q, src, ss, rs):
        def step(t, carry):
            o = dp_peer(t)
            stage[i, o, :, cols[c]] = src[tab[ROW_PLACE + q, o]]
            one(stage.at[i, o, :, cols[c]], gath.at[i, mine, cols[c]], ss, rs, o)
            return carry

        for p in far_order():
            step(p, 0)
        gath[i, mine, cols[c]] = src[tab[ROW_PLACE + q, d]]

    ag = []
    for c in range(CHUNKS):
        for p in (2, 3, 4, 5):
            rs[c][p].wait_recv()

        def add(j, carry, c=c):
            for at, pieces in ((0, (4, 3)), (few, (2, 5))):
                total = grad[tab[ROW_BLOCK, CAP * (at + j) + r], :, cols[c]].astype(jnp.float32)
                for p in pieces:
                    total += rs_recv[c, p, j].astype(jnp.float32)
                s_own[c][at + j] = total.astype(jnp.bfloat16)
            return carry

        lax.fori_loop(0, few, add, 0)
        ag.append(share((0, 1, 2 + c % 2), sums(c), ag_ss.at[c], ag_rs.at[c]))
        to_owners(0, c, r, s_own[c], pr_ss.at[c], pr_rs.at[c])

    def pass_sums_on(c):
        pass_on(ag[c], sums(c), ag_ss.at[c], ag_rs.at[c])

    def others(i, c):
        for p in ((2,), (3,), (4, 5))[i - 1]:
            ag[c][p].wait_recv()
        q = rep_of(reps - STEPS[i - 1])
        to_owners(i, c, q, s_recv[(i - 1) * CHUNKS + c], ot_ss.at[c, i - 1], ot_rs.at[c, i - 1])

    def from_neighbour(i, c):
        arrived = gath.at[0, :, cols[c]]
        return to_rep(i, arrived, gath.at[1 + i, :, cols[c]], ow_ss.at[c], ow_rs.at[c])

    pass_sums_on(0)
    others(1, 0)
    for c in range(1, CHUNKS):
        pass_sums_on(c)

    slot = (r - tab[ROW_START, d]) & 3
    for load in load_roots:
        load.wait()
    ow = []
    for c in range(CHUNKS):
        arrived = gath.at[0, pl.ds(0, rows * (devs - 1)), cols[c]]
        pltpu.make_async_copy(arrived, arrived, pr_rs.at[c]).wait()
        ow.append(from_neighbour(1 - c % 2, c))
        for m in range(0, width, tile):
            half[m : m + tile, cols[c]] = jnp.dot(
                lroot[slot, m : m + tile, :], gath[0, :, cols[c]], preferred_element_type=jnp.float32
            ).astype(jnp.bfloat16)
    grad_sq = jnp.zeros((1, 1), jnp.float32)
    dir_sq = jnp.zeros((1, 1), jnp.float32)
    for m in range(0, width, tile):
        piece = jnp.dot(half[m : m + tile, :], rroot[slot], preferred_element_type=jnp.float32)
        direct[m : m + tile, :] = piece
        dir_sq += jnp.sum(piece * piece, keepdims=True)
        g = gath[0, m : m + tile, :].astype(jnp.float32)
        grad_sq += jnp.sum(g * g, keepdims=True)
    scale = jnp.sqrt(grad_sq) / jnp.sqrt(dir_sq + EPS)
    for m in range(0, width, tile):
        upd[m : m + tile, :] = (direct[m : m + tile, :] * scale).astype(jnp.bfloat16)

    for c in range(CHUNKS):

        def homeward(t, carry, c=c):
            to = dp_peer(t)
            theirs = pl.ds(pl.multiple_of(to * rows, rows), rows)
            one(upd.at[theirs, cols[c]], back[c].at[d], bk_ss.at[c], bk_rs.at[c], to)
            return carry

        for p in far_order():
            homeward(p, 0)
        back[c][d] = upd[mine, cols[c]]

    others(3, 0)
    for c in range(1, CHUNKS):
        others(1 + c % 2, c)
        others(3, c)

    def gram(i):
        if i > 0:
            for c in range(CHUNKS):
                if i == 3 or i == 1 + c % 2:
                    arrived = gath.at[i, pl.ds(0, rows * (devs - 1)), cols[c]]
                    pltpu.make_async_copy(arrived, arrived, ot_rs.at[c, i - 1]).wait()
                else:
                    ow[c].wait_recv()
        for m in range(0, width, tile):
            sl = pl.ds(m, tile)
            left_gram[i, sl, :] = lax.dot_general(
                gath[i, sl, :], gath[i], (((1,), (1,)), ((), ())), preferred_element_type=jnp.float32
            )
            right_gram[i, sl, :] = lax.dot_general(
                gath[i, :, sl], gath[i], (((0,), (0,)), ((), ())), preferred_element_type=jnp.float32
            )

    gram(0)

    def steps(c):
        return lambda i, sl: uall.at[i, sl, :, cols[c]]

    au = []
    for c in range(CHUNKS):
        arrived = back[c].at[pl.ds(0, devs - 1)]
        pltpu.make_async_copy(arrived, arrived, bk_rs.at[c]).wait()

        def unpack(j, carry, c=c):
            uall[0, j, :, cols[c]] = back[c][tab[ROW_OWNER, CAP * j + r]]
            return carry

        lax.fori_loop(0, places, unpack, 0)
        au.append(share((0, 1, 2, 3), steps(c), au_ss.at[c], au_rs.at[c]))
    gram(1)
    for c in range(CHUNKS):
        pass_on(au[c], steps(c), au_ss.at[c], au_rs.at[c])

    gram(2)
    gram(3)

    for c in range(CHUNKS):
        for copy in rs[c] + list(ag[c].values()) + list(au[c].values()) + [ow[c]]:
            copy.wait_send()
        for i in (0, 1 + c % 2, 3):
            sent = stage.at[i, pl.ds(0, devs - 1), :, cols[c]]
            pltpu.make_async_copy(sent, sent, pr_ss.at[c] if i == 0 else ot_ss.at[c, i - 1]).wait()
        sent = back[c].at[pl.ds(0, devs - 1)]
        pltpu.make_async_copy(sent, sent, bk_ss.at[c]).wait()
        for p in (2, 3, 4, 5):
            au[c][p].wait_recv()
    for load in load_factors:
        load.wait()


def write_out(
    reps, tab_v, left_gram, right_gram, uall, lf, rf, update, left_out, right_out, tab, left_buf, right_buf, sems
):
    r = lax.axis_index("rep")
    d = lax.axis_index("dp")
    blocks, width = update.shape[0], lf.shape[2]
    tile = min(128, width)
    load = pltpu.make_async_copy(tab_v, tab, sems.at[0])
    load.start()
    load.wait()

    def buffer_of(q):
        step = lax.rem(r - q + reps, reps)
        return jnp.where(step < 2, step, 5 - step)

    start, count = tab[ROW_START, d], tab[ROW_COUNT, d]
    weight = (1.0 - DECAY) / width
    sides = ((lf, left_gram, left_buf, left_out), (rf, right_gram, right_buf, right_out))
    for s in range(CAP):
        valid = s < count
        i = buffer_of((start + s) & 3)
        for factor, gram, buf, out in sides:
            for m in range(0, width, tile):
                sl = pl.ds(m, tile)
                buf[s, sl, :] = DECAY * factor[s, sl, :] + jnp.where(valid, weight * gram[i, sl, :], 0.0)
                pltpu.make_async_copy(buf.at[s, sl], out.at[s, sl], sems.at[2]).start()

    def put(b, carry):
        pos = tab[ROW_POS, b]
        pltpu.make_async_copy(uall.at[buffer_of(pos & 3), pos >> 2], update.at[b], sems.at[1]).start()
        return carry

    lax.fori_loop(0, blocks, put, 0)
    pltpu.make_async_copy(left_buf, left_out, sems.at[2]).wait()
    pltpu.make_async_copy(right_buf, right_out, sems.at[2]).wait()
    pltpu.make_async_copy(uall, uall, sems.at[1]).wait()


def shards(reps, devs, gradient, owner, left_factor, right_factor, left_root, right_root):
    bf16, f32 = jnp.bfloat16, jnp.float32
    _, blocks, rows, width = gradient.shape
    places = blocks // reps
    part = width // CHUNKS
    any_spec = pl.BlockSpec(memory_space=pl.ANY)
    hbm_spec = pl.BlockSpec(memory_space=pltpu.HBM)
    vmem_spec = pl.BlockSpec(memory_space=pltpu.VMEM)
    dma = pltpu.SemaphoreType.DMA
    three = len(STEPS)
    tab, left_gram, right_gram, uall, lf, rf = pl.pallas_call(
        functools.partial(exchange, reps, devs),
        name="exchange",
        out_shape=[
            in_vmem((TAB_ROWS, 128), jnp.int32),
            in_vmem((CAP, width, width), f32),
            in_vmem((CAP, width, width), f32),
            in_vmem((CAP, places, rows, width), bf16),
            in_vmem((CAP, width, width), f32),
            in_vmem((CAP, width, width), f32),
        ],
        in_specs=[hbm_spec] * 6,
        out_specs=[vmem_spec] * 6,
        scratch_shapes=[
            pltpu.SMEM((TAB_ROWS, 128), jnp.int32),
            pltpu.VMEM((CAP, width, width), bf16),
            pltpu.VMEM((1, blocks), jnp.int32),
            pltpu.VMEM((blocks, rows, width), bf16),
            pltpu.VMEM((CAP, width, width), bf16),
            pltpu.VMEM((CAP, width, width), bf16),
            pltpu.VMEM((CHUNKS, PIECES, places // 2, rows, part), bf16),
            pltpu.VMEM((CHUNKS, PIECES, places // 2, rows, part), bf16),
            pltpu.VMEM((CAP, devs, rows, width), bf16),
            pltpu.VMEM((width, width), bf16),
            pltpu.VMEM((width, width), f32),
            pltpu.VMEM((width, width), bf16),
            [pltpu.VMEM((places, rows, part), bf16)] * CHUNKS,
            [pltpu.VMEM((places, rows, part), bf16)] * (CHUNKS * three),
            [pltpu.VMEM((devs, rows, part), bf16)] * CHUNKS,
            dma((7,)),
            dma((CHUNKS, PIECES)),
            dma((CHUNKS, PIECES)),
            dma((CHUNKS, PIECES)),
            dma((CHUNKS, PIECES)),
            dma((CHUNKS,)),
            dma((CHUNKS,)),
            dma((CHUNKS, three)),
            dma((CHUNKS, three)),
            dma((CHUNKS, PIECES)),
            dma((CHUNKS, PIECES)),
            dma((CHUNKS,)),
            dma((CHUNKS,)),
            dma((CHUNKS, PIECES)),
            dma((CHUNKS, PIECES)),
        ],
        compiler_params=pltpu.CompilerParams(
            collective_id=0, has_side_effects=True, vmem_limit_bytes=40 * 2**20
        ),
    )(in_hbm(owner.reshape(1, blocks)), *(in_hbm(x) for x in (gradient, left_factor, right_factor, left_root, right_root)))
    update, left_out, right_out = pl.pallas_call(
        functools.partial(write_out, reps),
        name="write_out",
        out_shape=[
            jax.ShapeDtypeStruct((blocks, rows, width), bf16),
            jax.ShapeDtypeStruct((CAP, width, width), f32),
            jax.ShapeDtypeStruct((CAP, width, width), f32),
        ],
        in_specs=[any_spec] + [vmem_spec] * 5,
        out_specs=[hbm_spec] * 3,
        scratch_shapes=[
            pltpu.SMEM((TAB_ROWS, 128), jnp.int32),
            pltpu.VMEM((CAP, width, width), f32),
            pltpu.VMEM((CAP, width, width), f32),
            dma((3,)),
        ],
        compiler_params=pltpu.CompilerParams(vmem_limit_bytes=24 * 2**20),
    )(tab, *(from_vmem(x) for x in (left_gram, right_gram, uall, lf, rf)))
    return update, left_out, right_out


def solution(mesh):
    in_specs = (
        P("rep", None, "dp", None),
        P(),
        P("dp", None, None),
        P("dp", None, None),
        P("dp", None, None),
        P("dp", None, None),
    )
    out_specs = (P(None, "dp", None), P("dp", None, None), P("dp", None, None))
    body = functools.partial(shards, mesh.shape["rep"], mesh.shape["dp"])
    return jax.shard_map(body, mesh=mesh, in_specs=in_specs, out_specs=out_specs, check_vma=False)
```

```python
import functools

import jax
import jax.numpy as jnp
from jax import lax
from jax.experimental import pallas as pl
from jax.experimental.pallas import tpu as pltpu
from jax.sharding import PartitionSpec as P

MESH = pl.DeviceIdType.MESH
CAP = 4
DECAY = 0.9
EPS = 1e-06
CHUNKS = 2
PIECES = 6
STEPS = (1, 3, 2)
TAB_ROWS = 16
ROW_BLOCK, ROW_POS, ROW_OWNER, ROW_START, ROW_COUNT, ROW_PLACE = 0, 1, 2, 3, 4, 5


def far_order():
    near = {0: 0, 1: 1, 2: 2, 3: 1}
    every = [(z, x, c) for z in range(4) for x in range(4) for c in range(2) if (z, x, c) != (0, 0, 0)]
    return sorted(every, key=lambda p: -(near[p[0]] + near[p[1]]))


def in_vmem(shape, dtype):
    return pltpu.VMEM(shape, dtype)


def in_hbm(x):
    return pltpu.with_memory_space_constraint(x, pltpu.HBM)


def from_vmem(x):
    return pltpu.with_memory_space_constraint(x, pltpu.VMEM)


def fill_tables(owner_ref, tab_ref):
    blocks = owner_ref.shape[1]
    lanes = tab_ref.shape[1]
    b = lax.broadcasted_iota(jnp.int32, (blocks, lanes), 0)
    c = lax.broadcasted_iota(jnp.int32, (blocks, lanes), 1)

    def down(x):
        return jnp.sum(x, axis=0, keepdims=True)

    inside = c < blocks
    row = jnp.broadcast_to(jnp.pad(owner_ref[...], ((0, 0), (0, lanes - blocks))), (blocks, lanes))
    col = jnp.sum(jnp.where(b == c, row, 0), axis=1, keepdims=True)
    col = jnp.broadcast_to(col, (blocks, lanes))
    before = (row < col) | ((row == col) & (c < b))
    pos_col = jnp.sum(jnp.where(before & inside, 1, 0), axis=1, keepdims=True)
    pos_col = jnp.broadcast_to(pos_col, (blocks, lanes))
    after = (col < row) | ((col == row) & (b < c))
    pos_row = down(jnp.where(after, 1, 0))
    here = pos_col == c
    start = down(jnp.where(col < c, 1, 0))
    count = down(jnp.where(col == c, 1, 0))
    tab_ref[ROW_BLOCK : ROW_BLOCK + 1, :] = down(jnp.where(here, b, 0))
    tab_ref[ROW_POS : ROW_POS + 1, :] = pos_row
    tab_ref[ROW_OWNER : ROW_OWNER + 1, :] = down(jnp.where(here, col, 0))
    tab_ref[ROW_START : ROW_START + 1, :] = start
    tab_ref[ROW_COUNT : ROW_COUNT + 1, :] = count
    for q in range(CAP):
        slot = (q - start) & 3
        place = jnp.where(slot < count, (start + slot) >> 2, 0)
        tab_ref[ROW_PLACE + q : ROW_PLACE + q + 1, :] = place
    rest = ROW_PLACE + CAP
    tab_ref[rest:, :] = jnp.zeros((TAB_ROWS - rest, lanes), jnp.int32)


def exchange(
    reps, devs, owner_hbm, grad_hbm, lf_hbm, rf_hbm, lr_hbm, rr_hbm,
    tab_out, left_gram, right_gram, uall, lf_out, rf_out,
    tab, gath, owner, grad, lroot, rroot, rs_send, rs_recv, stage, half, direct, upd, s_own, s_recv, back,
    loc_sem, rs_ss, rs_rs, ag_ss, ag_rs, pr_ss, pr_rs, ot_ss, ot_rs, ow_ss, ow_rs, bk_ss, bk_rs, au_ss, au_rs,
):
    r = lax.axis_index("rep")
    d = lax.axis_index("dp")
    places, rows, width = s_own[0].shape[0], grad.shape[1], grad.shape[2]
    part = width // CHUNKS
    cols = [pl.ds(c * part, part) for c in range(CHUNKS)]
    tile = min(256, width)
    mine = pl.ds(pl.multiple_of(d * rows, rows), rows)
    few = places // 2
    first, last = pl.ds(0, few), pl.ds(few, few)

    def rep_of(k):
        return lax.rem(r + k, reps)

    def dp_peer(t):
        if not isinstance(t, tuple):
            return lax.rem(d + t, devs)
        dz, dx, dc = t
        z, x, c = d // 8, lax.rem(d // 2, 4), lax.rem(d, 2)
        return lax.rem(z + dz, 4) * 8 + lax.rem(x + dx, 4) * 2 + lax.rem(c + dc, 2)

    def local(src, dst, i):
        return pltpu.make_async_copy(src, dst, loc_sem.at[i])

    load_owner, load_grad = local(owner_hbm, owner, 0), local(grad_hbm.at[0], grad, 1)
    load_roots = [local(lr_hbm, lroot, 2), local(rr_hbm, rroot, 3)]
    load_factors = [local(lf_hbm, lf_out, 4), local(rf_hbm, rf_out, 5)]
    load_owner.start()
    load_grad.start()

    barrier = pltpu.get_barrier_semaphore()
    for k in STEPS:
        pl.semaphore_signal(barrier, inc=1, device_id=(rep_of(k), d), device_id_type=MESH)

    def greet(t, carry):
        pl.semaphore_signal(barrier, inc=1, device_id=(r, dp_peer(t)), device_id_type=MESH)
        return carry

    for p in far_order():
        greet(p, 0)

    load_owner.wait()
    fill_tables(owner, tab_out)
    to_scalars = local(tab_out, tab, 6)
    to_scalars.start()
    to_scalars.wait()
    load_grad.wait()

    def to_rep(piece, src, dst, ss, rs):
        copy = pltpu.make_async_remote_copy(
            src_ref=src,
            dst_ref=dst,
            send_sem=ss.at[piece],
            recv_sem=rs.at[piece],
            device_id=(rep_of(1 if piece % 2 == 0 else reps - 1), d),
            device_id_type=MESH,
        )
        copy.start()
        return copy

    packing = ((2, 0), (2, few), (1, few), (reps - 1, 0), (1, 0), (reps - 1, few))

    def pack(pieces, c):
        def step(j, carry):
            for p in pieces:
                k, at = packing[p]
                block = tab[ROW_BLOCK, CAP * (at + j) + rep_of(k)]
                rows_here = grad[block, :, cols[c]]
                if p >= 4:
                    both = rows_here.astype(jnp.float32) + rs_recv[c, p - 4, j].astype(jnp.float32)
                    rows_here = both.astype(jnp.bfloat16)
                rs_send[c, p, j] = rows_here
            return carry

        lax.fori_loop(0, few, step, 0, unroll=True)

    def send_sums(p, c):
        return to_rep(p, rs_send.at[c, p], rs_recv.at[c, p], rs_ss.at[c], rs_rs.at[c])

    for c in range(CHUNKS):
        pack((0, 1, 2, 3), c)
    pl.semaphore_wait(barrier, reps - 1 + devs - 1)
    rs = [{p: send_sums(p, c) for p in (range(4) if c == 0 else range(2))} for c in range(CHUNKS)]
    for load in load_roots + load_factors:
        load.start()
    for c in range(CHUNKS):
        for p in (4, 5):
            rs[c][p - 4].wait_recv()
            pack((p,), c)
            rs[c][p] = send_sums(p, c)
        if c == 0:
            for e in range(1, CHUNKS):
                for p in (2, 3):
                    rs[e][p] = send_sums(p, e)

    def share(pieces, buf, ss, rs):
        halves = (first, last, last, first)
        return {p: to_rep(p, buf(0, halves[p]), buf(1 + p % 2, halves[p]), ss, rs) for p in pieces}

    def pass_on(copies, buf, ss, rs):
        copies[0].wait_recv()
        copies[4] = to_rep(4, buf(1, first), buf(3, first), ss, rs)
        copies[1].wait_recv()
        copies[5] = to_rep(5, buf(2, last), buf(3, last), ss, rs)

    def sums(c):
        return lambda i, sl: (s_own[c] if i == 0 else s_recv[(i - 1) * CHUNKS + c]).at[sl]

    def one(src, dst, ss, rs, to):
        pltpu.make_async_remote_copy(
            src_ref=src, dst_ref=dst, send_sem=ss, recv_sem=rs, device_id=(r, to), device_id_type=MESH
        ).start()

    def to_owners(i, c, q, src, ss, rs):
        def step(t, carry):
            o = dp_peer(t)
            stage[i, o, :, cols[c]] = src[tab[ROW_PLACE + q, o]]
            one(stage.at[i, o, :, cols[c]], gath.at[i, mine, cols[c]], ss, rs, o)
            return carry

        for p in far_order():
            step(p, 0)
        gath[i, mine, cols[c]] = src[tab[ROW_PLACE + q, d]]

    ag = []
    for c in range(CHUNKS):
        for p in (2, 3, 4, 5):
            rs[c][p].wait_recv()

        def add(j, carry, c=c):
            for at, pieces in ((0, (4, 3)), (few, (2, 5))):
                total = grad[tab[ROW_BLOCK, CAP * (at + j) + r], :, cols[c]].astype(jnp.float32)
                for p in pieces:
                    total += rs_recv[c, p, j].astype(jnp.float32)
                s_own[c][at + j] = total.astype(jnp.bfloat16)
            return carry

        lax.fori_loop(0, few, add, 0, unroll=True)
        ag.append(share((0, 1, 2 + c % 2), sums(c), ag_ss.at[c], ag_rs.at[c]) if c == 0 else {})
        to_owners(0, c, r, s_own[c], pr_ss.at[c], pr_rs.at[c])
        if c > 0:
            ag[c] = share((0, 1, 2 + c % 2), sums(c), ag_ss.at[c], ag_rs.at[c])

    def pass_sums_on(c):
        pass_on(ag[c], sums(c), ag_ss.at[c], ag_rs.at[c])

    def others(i, c):
        for p in ((2,), (3,), (4, 5))[i - 1]:
            ag[c][p].wait_recv()
        q = rep_of(reps - STEPS[i - 1])
        to_owners(i, c, q, s_recv[(i - 1) * CHUNKS + c], ot_ss.at[c, i - 1], ot_rs.at[c, i - 1])

    def from_neighbour(i, c):
        arrived = gath.at[0, :, cols[c]]
        return to_rep(i, arrived, gath.at[1 + i, :, cols[c]], ow_ss.at[c], ow_rs.at[c])

    pass_sums_on(0)
    others(1, 0)
    for c in range(1, CHUNKS):
        pass_sums_on(c)

    slot = (r - tab[ROW_START, d]) & 3
    for load in load_roots:
        load.wait()
    ow = []
    for c in range(CHUNKS):
        arrived = gath.at[0, pl.ds(0, rows * (devs - 1)), cols[c]]
        pltpu.make_async_copy(arrived, arrived, pr_rs.at[c]).wait()
        ow.append(from_neighbour(1 - c % 2, c))
        for m in range(0, width, tile):
            half[m : m + tile, cols[c]] = jnp.dot(
                lroot[slot, m : m + tile, :], gath[0, :, cols[c]], preferred_element_type=jnp.float32
            ).astype(jnp.bfloat16)
    grad_sq = jnp.zeros((1, 1), jnp.float32)
    dir_sq = jnp.zeros((1, 1), jnp.float32)
    for m in range(0, width, tile):
        piece = jnp.dot(half[m : m + tile, :], rroot[slot], preferred_element_type=jnp.float32)
        direct[m : m + tile, :] = piece
        dir_sq += jnp.sum(piece * piece, keepdims=True)
        g = gath[0, m : m + tile, :].astype(jnp.float32)
        grad_sq += jnp.sum(g * g, keepdims=True)
    scale = jnp.sqrt(grad_sq) / jnp.sqrt(dir_sq + EPS)
    for m in range(0, width, tile):
        upd[m : m + tile, :] = (direct[m : m + tile, :] * scale).astype(jnp.bfloat16)

    for c in range(CHUNKS):

        def homeward(t, carry, c=c):
            to = dp_peer(t)
            theirs = pl.ds(pl.multiple_of(to * rows, rows), rows)
            one(upd.at[theirs, cols[c]], back[c].at[d], bk_ss.at[c], bk_rs.at[c], to)
            return carry

        for p in far_order():
            homeward(p, 0)
        back[c][d] = upd[mine, cols[c]]

    others(3, 0)
    for c in range(1, CHUNKS):
        others(1 + c % 2, c)
        others(3, c)

    def gram(i):
        if i > 0:
            for c in range(CHUNKS):
                if i == 3 or i == 1 + c % 2:
                    arrived = gath.at[i, pl.ds(0, rows * (devs - 1)), cols[c]]
                    pltpu.make_async_copy(arrived, arrived, ot_rs.at[c, i - 1]).wait()
                else:
                    ow[c].wait_recv()
        for m in range(0, width, tile):
            sl = pl.ds(m, tile)
            left_gram[i, sl, :] = lax.dot_general(
                gath[i, sl, :], gath[i], (((1,), (1,)), ((), ())), preferred_element_type=jnp.float32
            )
            right_gram[i, sl, :] = lax.dot_general(
                gath[i, :, sl], gath[i], (((0,), (0,)), ((), ())), preferred_element_type=jnp.float32
            )

    gram(0)

    def steps(c):
        return lambda i, sl: uall.at[i, sl, :, cols[c]]

    au = []
    for c in range(CHUNKS):
        arrived = back[c].at[pl.ds(0, devs - 1)]
        pltpu.make_async_copy(arrived, arrived, bk_rs.at[c]).wait()

        def unpack(j, carry, c=c):
            uall[0, j, :, cols[c]] = back[c][tab[ROW_OWNER, CAP * j + r]]
            return carry

        lax.fori_loop(0, places, unpack, 0, unroll=True)
        au.append(share((0, 1, 2, 3) if c == 0 else (0, 1), steps(c), au_ss.at[c], au_rs.at[c]))
    for c in range(CHUNKS):
        if c > 0:
            au[c].update(share((2, 3), steps(c), au_ss.at[c], au_rs.at[c]))
        pass_on(au[c], steps(c), au_ss.at[c], au_rs.at[c])

    gram(1)
    gram(2)
    gram(3)

    for c in range(CHUNKS):
        for copy in list(rs[c].values()) + list(ag[c].values()) + list(au[c].values()) + [ow[c]]:
            copy.wait_send()
        for i in (0, 1 + c % 2, 3):
            sent = stage.at[i, pl.ds(0, devs - 1), :, cols[c]]
            pltpu.make_async_copy(sent, sent, pr_ss.at[c] if i == 0 else ot_ss.at[c, i - 1]).wait()
        sent = back[c].at[pl.ds(0, devs - 1)]
        pltpu.make_async_copy(sent, sent, bk_ss.at[c]).wait()
        for p in (2, 3, 4, 5):
            au[c][p].wait_recv()
    for load in load_factors:
        load.wait()


def write_out(
    reps, tab_v, left_gram, right_gram, uall, lf, rf, update, left_out, right_out, tab, left_buf, right_buf, sems
):
    r = lax.axis_index("rep")
    d = lax.axis_index("dp")
    blocks, width = update.shape[0], lf.shape[2]
    tile = min(128, width)
    load = pltpu.make_async_copy(tab_v, tab, sems.at[0])
    load.start()
    load.wait()

    def buffer_of(q):
        step = lax.rem(r - q + reps, reps)
        return jnp.where(step < 2, step, 5 - step)

    start, count = tab[ROW_START, d], tab[ROW_COUNT, d]
    weight = (1.0 - DECAY) / width
    sides = ((lf, left_gram, left_buf, left_out), (rf, right_gram, right_buf, right_out))
    for s in range(CAP):
        valid = s < count
        i = buffer_of((start + s) & 3)
        for factor, gram, buf, out in sides:
            for m in range(0, width, tile):
                sl = pl.ds(m, tile)
                buf[s, sl, :] = DECAY * factor[s, sl, :] + jnp.where(valid, weight * gram[i, sl, :], 0.0)
                pltpu.make_async_copy(buf.at[s, sl], out.at[s, sl], sems.at[2]).start()

    def put(b, carry):
        pos = tab[ROW_POS, b]
        pltpu.make_async_copy(uall.at[buffer_of(pos & 3), pos >> 2], update.at[b], sems.at[1]).start()
        return carry

    lax.fori_loop(0, blocks, put, 0)
    pltpu.make_async_copy(left_buf, left_out, sems.at[2]).wait()
    pltpu.make_async_copy(right_buf, right_out, sems.at[2]).wait()
    pltpu.make_async_copy(uall, uall, sems.at[1]).wait()


def shards(reps, devs, gradient, owner, left_factor, right_factor, left_root, right_root):
    bf16, f32 = jnp.bfloat16, jnp.float32
    _, blocks, rows, width = gradient.shape
    places = blocks // reps
    part = width // CHUNKS
    any_spec = pl.BlockSpec(memory_space=pl.ANY)
    hbm_spec = pl.BlockSpec(memory_space=pltpu.HBM)
    vmem_spec = pl.BlockSpec(memory_space=pltpu.VMEM)
    dma = pltpu.SemaphoreType.DMA
    three = len(STEPS)
    tab, left_gram, right_gram, uall, lf, rf = pl.pallas_call(
        functools.partial(exchange, reps, devs),
        name="exchange",
        out_shape=[
            in_vmem((TAB_ROWS, 128), jnp.int32),
            in_vmem((CAP, width, width), f32),
            in_vmem((CAP, width, width), f32),
            in_vmem((CAP, places, rows, width), bf16),
            in_vmem((CAP, width, width), f32),
            in_vmem((CAP, width, width), f32),
        ],
        in_specs=[hbm_spec] * 6,
        out_specs=[vmem_spec] * 6,
        scratch_shapes=[
            pltpu.SMEM((TAB_ROWS, 128), jnp.int32),
            pltpu.VMEM((CAP, width, width), bf16),
            pltpu.VMEM((1, blocks), jnp.int32),
            pltpu.VMEM((blocks, rows, width), bf16),
            pltpu.VMEM((CAP, width, width), bf16),
            pltpu.VMEM((CAP, width, width), bf16),
            pltpu.VMEM((CHUNKS, PIECES, places // 2, rows, part), bf16),
            pltpu.VMEM((CHUNKS, PIECES, places // 2, rows, part), bf16),
            pltpu.VMEM((CAP, devs, rows, width), bf16),
            pltpu.VMEM((width, width), bf16),
            pltpu.VMEM((width, width), f32),
            pltpu.VMEM((width, width), bf16),
            [pltpu.VMEM((places, rows, part), bf16)] * CHUNKS,
            [pltpu.VMEM((places, rows, part), bf16)] * (CHUNKS * three),
            [pltpu.VMEM((devs, rows, part), bf16)] * CHUNKS,
            dma((7,)),
            dma((CHUNKS, PIECES)),
            dma((CHUNKS, PIECES)),
            dma((CHUNKS, PIECES)),
            dma((CHUNKS, PIECES)),
            dma((CHUNKS,)),
            dma((CHUNKS,)),
            dma((CHUNKS, three)),
            dma((CHUNKS, three)),
            dma((CHUNKS, PIECES)),
            dma((CHUNKS, PIECES)),
            dma((CHUNKS,)),
            dma((CHUNKS,)),
            dma((CHUNKS, PIECES)),
            dma((CHUNKS, PIECES)),
        ],
        compiler_params=pltpu.CompilerParams(
            collective_id=0, has_side_effects=True, vmem_limit_bytes=40 * 2**20
        ),
    )(in_hbm(owner.reshape(1, blocks)), *(in_hbm(x) for x in (gradient, left_factor, right_factor, left_root, right_root)))
    update, left_out, right_out = pl.pallas_call(
        functools.partial(write_out, reps),
        name="write_out",
        out_shape=[
            jax.ShapeDtypeStruct((blocks, rows, width), bf16),
            jax.ShapeDtypeStruct((CAP, width, width), f32),
            jax.ShapeDtypeStruct((CAP, width, width), f32),
        ],
        in_specs=[any_spec] + [vmem_spec] * 5,
        out_specs=[hbm_spec] * 3,
        scratch_shapes=[
            pltpu.SMEM((TAB_ROWS, 128), jnp.int32),
            pltpu.VMEM((CAP, width, width), f32),
            pltpu.VMEM((CAP, width, width), f32),
            dma((3,)),
        ],
        compiler_params=pltpu.CompilerParams(vmem_limit_bytes=24 * 2**20),
    )(tab, *(from_vmem(x) for x in (left_gram, right_gram, uall, lf, rf)))
    return update, left_out, right_out


def solution(mesh):
    in_specs = (
        P("rep", None, "dp", None),
        P(),
        P("dp", None, None),
        P("dp", None, None),
        P("dp", None, None),
        P("dp", None, None),
    )
    out_specs = (P(None, "dp", None), P("dp", None, None), P("dp", None, None))
    body = functools.partial(shards, mesh.shape["rep"], mesh.shape["dp"])
    return jax.shard_map(body, mesh=mesh, in_specs=in_specs, out_specs=out_specs, check_vma=False)
```

```python
import functools

import jax
import jax.numpy as jnp
from jax import lax
from jax.experimental import pallas as pl
from jax.experimental.pallas import tpu as pltpu
from jax.sharding import PartitionSpec as P

MESH = pl.DeviceIdType.MESH
CAP = 4
DECAY = 0.9
EPS = 1e-06
CHUNKS = 2
BACK = (0, 256, 512)
PIECES = 6
STEPS = (1, 3, 2)
TAB_ROWS = 16
ROW_BLOCK, ROW_POS, ROW_OWNER, ROW_START, ROW_COUNT, ROW_PLACE = 0, 1, 2, 3, 4, 5


def far_order():
    near = {0: 0, 1: 1, 2: 2, 3: 1}
    every = [(z, x, c) for z in range(4) for x in range(4) for c in range(2) if (z, x, c) != (0, 0, 0)]
    return sorted(every, key=lambda p: -(near[p[0]] + near[p[1]]))


def in_vmem(shape, dtype):
    return pltpu.VMEM(shape, dtype)


def in_hbm(x):
    return pltpu.with_memory_space_constraint(x, pltpu.HBM)


def from_vmem(x):
    return pltpu.with_memory_space_constraint(x, pltpu.VMEM)


def fill_tables(owner_ref, tab_ref):
    blocks = owner_ref.shape[1]
    lanes = tab_ref.shape[1]
    b = lax.broadcasted_iota(jnp.int32, (blocks, lanes), 0)
    c = lax.broadcasted_iota(jnp.int32, (blocks, lanes), 1)

    def down(x):
        return jnp.sum(x, axis=0, keepdims=True)

    inside = c < blocks
    row = jnp.broadcast_to(jnp.pad(owner_ref[...], ((0, 0), (0, lanes - blocks))), (blocks, lanes))
    col = jnp.sum(jnp.where(b == c, row, 0), axis=1, keepdims=True)
    col = jnp.broadcast_to(col, (blocks, lanes))
    before = (row < col) | ((row == col) & (c < b))
    pos_col = jnp.sum(jnp.where(before & inside, 1, 0), axis=1, keepdims=True)
    pos_col = jnp.broadcast_to(pos_col, (blocks, lanes))
    after = (col < row) | ((col == row) & (b < c))
    pos_row = down(jnp.where(after, 1, 0))
    here = pos_col == c
    start = down(jnp.where(col < c, 1, 0))
    count = down(jnp.where(col == c, 1, 0))
    tab_ref[ROW_BLOCK : ROW_BLOCK + 1, :] = down(jnp.where(here, b, 0))
    tab_ref[ROW_POS : ROW_POS + 1, :] = pos_row
    tab_ref[ROW_OWNER : ROW_OWNER + 1, :] = down(jnp.where(here, col, 0))
    tab_ref[ROW_START : ROW_START + 1, :] = start
    tab_ref[ROW_COUNT : ROW_COUNT + 1, :] = count
    for q in range(CAP):
        slot = (q - start) & 3
        place = jnp.where(slot < count, (start + slot) >> 2, 0)
        tab_ref[ROW_PLACE + q : ROW_PLACE + q + 1, :] = place
    rest = ROW_PLACE + CAP
    tab_ref[rest:, :] = jnp.zeros((TAB_ROWS - rest, lanes), jnp.int32)


def exchange(
    reps, devs, owner_hbm, grad_hbm, lf_hbm, rf_hbm, lr_hbm, rr_hbm,
    tab_out, left_gram, right_gram, uall, lf_out, rf_out,
    tab, gath, owner, grad, lroot, rroot, rs_send, rs_recv, stage, half, direct, upd, s_own, s_recv, back,
    loc_sem, rs_ss, rs_rs, ag_ss, ag_rs, pr_ss, pr_rs, ot_ss, ot_rs, ow_ss, ow_rs, bk_ss, bk_rs, au_ss, au_rs,
):
    r = lax.axis_index("rep")
    d = lax.axis_index("dp")
    places, rows, width = s_own[0].shape[0], grad.shape[1], grad.shape[2]
    part = width // CHUNKS
    cols = [pl.ds(c * part, part) for c in range(CHUNKS)]
    bcols = [pl.ds(b * width // BACK[-1], (e - b) * width // BACK[-1]) for b, e in zip(BACK, BACK[1:])]
    tile = min(256, width)
    mine = pl.ds(pl.multiple_of(d * rows, rows), rows)
    few = places // 2
    first, last = pl.ds(0, few), pl.ds(few, few)

    def rep_of(k):
        return lax.rem(r + k, reps)

    def dp_peer(t):
        if not isinstance(t, tuple):
            return lax.rem(d + t, devs)
        dz, dx, dc = t
        z, x, c = d // 8, lax.rem(d // 2, 4), lax.rem(d, 2)
        return lax.rem(z + dz, 4) * 8 + lax.rem(x + dx, 4) * 2 + lax.rem(c + dc, 2)

    def local(src, dst, i):
        return pltpu.make_async_copy(src, dst, loc_sem.at[i])

    load_owner, load_grad = local(owner_hbm, owner, 0), local(grad_hbm.at[0], grad, 1)
    load_roots = [local(lr_hbm, lroot, 2), local(rr_hbm, rroot, 3)]
    load_factors = [local(lf_hbm, lf_out, 4), local(rf_hbm, rf_out, 5)]
    load_owner.start()
    load_grad.start()

    barrier = pltpu.get_barrier_semaphore()
    for k in STEPS:
        pl.semaphore_signal(barrier, inc=1, device_id=(rep_of(k), d), device_id_type=MESH)

    def greet(t, carry):
        pl.semaphore_signal(barrier, inc=1, device_id=(r, dp_peer(t)), device_id_type=MESH)
        return carry

    for p in far_order():
        greet(p, 0)

    load_owner.wait()
    fill_tables(owner, tab_out)
    to_scalars = local(tab_out, tab, 6)
    to_scalars.start()
    to_scalars.wait()
    load_grad.wait()

    def to_rep(piece, src, dst, ss, rs):
        copy = pltpu.make_async_remote_copy(
            src_ref=src,
            dst_ref=dst,
            send_sem=ss.at[piece],
            recv_sem=rs.at[piece],
            device_id=(rep_of(1 if piece % 2 == 0 else reps - 1), d),
            device_id_type=MESH,
        )
        copy.start()
        return copy

    packing = ((2, 0), (2, few), (1, few), (reps - 1, 0), (1, 0), (reps - 1, few))

    def pack(pieces, c):
        def step(j, carry):
            for p in pieces:
                k, at = packing[p]
                block = tab[ROW_BLOCK, CAP * (at + j) + rep_of(k)]
                rows_here = grad[block, :, cols[c]]
                if p >= 4:
                    both = rows_here.astype(jnp.float32) + rs_recv[c, p - 4, j].astype(jnp.float32)
                    rows_here = both.astype(jnp.bfloat16)
                rs_send[c, p, j] = rows_here
            return carry

        lax.fori_loop(0, few, step, 0, unroll=True)

    def send_sums(p, c):
        return to_rep(p, rs_send.at[c, p], rs_recv.at[c, p], rs_ss.at[c], rs_rs.at[c])

    for c in range(CHUNKS):
        pack((0, 1, 2, 3), c)
    pl.semaphore_wait(barrier, reps - 1 + devs - 1)
    rs = [{p: send_sums(p, c) for p in (range(4) if c == 0 else range(2))} for c in range(CHUNKS)]
    for load in load_roots + load_factors:
        load.start()
    for c in range(CHUNKS):
        for p in (4, 5):
            rs[c][p - 4].wait_recv()
            pack((p,), c)
            rs[c][p] = send_sums(p, c)
        if c == 0:
            for e in range(1, CHUNKS):
                for p in (2, 3):
                    rs[e][p] = send_sums(p, e)

    def share(pieces, buf, ss, rs):
        halves = (first, last, last, first)
        return {p: to_rep(p, buf(0, halves[p]), buf(1 + p % 2, halves[p]), ss, rs) for p in pieces}

    def pass_on(copies, buf, ss, rs):
        copies[0].wait_recv()
        copies[4] = to_rep(4, buf(1, first), buf(3, first), ss, rs)
        copies[1].wait_recv()
        copies[5] = to_rep(5, buf(2, last), buf(3, last), ss, rs)

    def sums(c):
        return lambda i, sl: (s_own[c] if i == 0 else s_recv[(i - 1) * CHUNKS + c]).at[sl]

    def one(src, dst, ss, rs, to):
        pltpu.make_async_remote_copy(
            src_ref=src, dst_ref=dst, send_sem=ss, recv_sem=rs, device_id=(r, to), device_id_type=MESH
        ).start()

    def to_owners(i, c, q, src, ss, rs):
        def step(t, carry):
            o = dp_peer(t)
            stage[i, o, :, cols[c]] = src[tab[ROW_PLACE + q, o]]
            one(stage.at[i, o, :, cols[c]], gath.at[i, mine, cols[c]], ss, rs, o)
            return carry

        for p in far_order():
            step(p, 0)
        gath[i, mine, cols[c]] = src[tab[ROW_PLACE + q, d]]

    ag = []
    for c in range(CHUNKS):
        for p in (2, 3, 4, 5):
            rs[c][p].wait_recv()

        def add(j, carry, c=c):
            for at, pieces in ((0, (4, 3)), (few, (2, 5))):
                total = grad[tab[ROW_BLOCK, CAP * (at + j) + r], :, cols[c]].astype(jnp.float32)
                for p in pieces:
                    total += rs_recv[c, p, j].astype(jnp.float32)
                s_own[c][at + j] = total.astype(jnp.bfloat16)
            return carry

        lax.fori_loop(0, few, add, 0, unroll=True)
        ag.append(share((0, 1, 2 + c % 2), sums(c), ag_ss.at[c], ag_rs.at[c]) if c == 0 else {})
        to_owners(0, c, r, s_own[c], pr_ss.at[c], pr_rs.at[c])
        if c > 0:
            ag[c] = share((0, 1, 2 + c % 2), sums(c), ag_ss.at[c], ag_rs.at[c])

    def pass_sums_on(c):
        pass_on(ag[c], sums(c), ag_ss.at[c], ag_rs.at[c])

    def others(i, c):
        for p in ((2,), (3,), (4, 5))[i - 1]:
            ag[c][p].wait_recv()
        q = rep_of(reps - STEPS[i - 1])
        to_owners(i, c, q, s_recv[(i - 1) * CHUNKS + c], ot_ss.at[c, i - 1], ot_rs.at[c, i - 1])

    def from_neighbour(i, c):
        arrived = gath.at[0, :, cols[c]]
        return to_rep(i, arrived, gath.at[1 + i, :, cols[c]], ow_ss.at[c], ow_rs.at[c])

    pass_sums_on(0)
    others(1, 0)
    for c in range(1, CHUNKS):
        pass_sums_on(c)

    slot = (r - tab[ROW_START, d]) & 3
    for load in load_roots:
        load.wait()
    ow = []
    for c in range(CHUNKS):
        arrived = gath.at[0, pl.ds(0, rows * (devs - 1)), cols[c]]
        pltpu.make_async_copy(arrived, arrived, pr_rs.at[c]).wait()
        ow.append(from_neighbour(1 - c % 2, c))
        for m in range(0, width, tile):
            half[m : m + tile, cols[c]] = jnp.dot(
                lroot[slot, m : m + tile, :], gath[0, :, cols[c]], preferred_element_type=jnp.float32
            ).astype(jnp.bfloat16)
    grad_sq = jnp.zeros((1, 1), jnp.float32)
    dir_sq = jnp.zeros((1, 1), jnp.float32)
    for m in range(0, width, tile):
        piece = jnp.dot(half[m : m + tile, :], rroot[slot], preferred_element_type=jnp.float32)
        direct[m : m + tile, :] = piece
        dir_sq += jnp.sum(piece * piece, keepdims=True)
        g = gath[0, m : m + tile, :].astype(jnp.float32)
        grad_sq += jnp.sum(g * g, keepdims=True)
    scale = jnp.sqrt(grad_sq) / jnp.sqrt(dir_sq + EPS)
    for m in range(0, width, tile):
        upd[m : m + tile, :] = (direct[m : m + tile, :] * scale).astype(jnp.bfloat16)

    for c in range(len(bcols)):

        def homeward(t, carry, c=c):
            to = dp_peer(t)
            theirs = pl.ds(pl.multiple_of(to * rows, rows), rows)
            one(upd.at[theirs, bcols[c]], back[c].at[d], bk_ss.at[c], bk_rs.at[c], to)
            return carry

        for p in far_order():
            homeward(p, 0)
        back[c][d] = upd[mine, bcols[c]]

    for c in range(1, CHUNKS):
        others(1 + c % 2, c)
    others(3, 0)
    for c in range(1, CHUNKS):
        others(3, c)

    def gram(i):
        if i > 0:
            for c in range(CHUNKS):
                if i == 3 or i == 1 + c % 2:
                    arrived = gath.at[i, pl.ds(0, rows * (devs - 1)), cols[c]]
                    pltpu.make_async_copy(arrived, arrived, ot_rs.at[c, i - 1]).wait()
                else:
                    ow[c].wait_recv()
        for m in range(0, width, tile):
            sl = pl.ds(m, tile)
            left_gram[i, sl, :] = lax.dot_general(
                gath[i, sl, :], gath[i], (((1,), (1,)), ((), ())), preferred_element_type=jnp.float32
            )
            right_gram[i, sl, :] = lax.dot_general(
                gath[i, :, sl], gath[i], (((0,), (0,)), ((), ())), preferred_element_type=jnp.float32
            )

    gram(0)

    gram(1)

    def steps(c):
        return lambda i, sl: uall.at[i, sl, :, bcols[c]]

    au = []
    for c in range(len(bcols)):
        arrived = back[c].at[pl.ds(0, devs - 1)]
        pltpu.make_async_copy(arrived, arrived, bk_rs.at[c]).wait()

        def unpack(j, carry, c=c):
            uall[0, j, :, bcols[c]] = back[c][tab[ROW_OWNER, CAP * j + r]]
            return carry

        lax.fori_loop(0, places, unpack, 0, unroll=True)
        au.append(share((0, 1), steps(c), au_ss.at[c], au_rs.at[c]))
        if c > 0:
            pass_on(au[c - 1], steps(c - 1), au_ss.at[c - 1], au_rs.at[c - 1])
        au[c].update(share((2, 3), steps(c), au_ss.at[c], au_rs.at[c]))
    pass_on(au[-1], steps(len(bcols) - 1), au_ss.at[len(bcols) - 1], au_rs.at[len(bcols) - 1])
    gram(2)
    gram(3)

    for c in range(CHUNKS):
        for copy in list(rs[c].values()) + list(ag[c].values()) + [ow[c]]:
            copy.wait_send()
        for i in (0, 1 + c % 2, 3):
            sent = stage.at[i, pl.ds(0, devs - 1), :, cols[c]]
            pltpu.make_async_copy(sent, sent, pr_ss.at[c] if i == 0 else ot_ss.at[c, i - 1]).wait()
    for c in range(len(bcols)):
        for copy in au[c].values():
            copy.wait_send()
        sent = back[c].at[pl.ds(0, devs - 1)]
        pltpu.make_async_copy(sent, sent, bk_ss.at[c]).wait()
        for p in (2, 3, 4, 5):
            au[c][p].wait_recv()
    for load in load_factors:
        load.wait()


def write_out(
    reps, tab_v, left_gram, right_gram, uall, lf, rf, update, left_out, right_out, tab, left_buf, right_buf, sems
):
    r = lax.axis_index("rep")
    d = lax.axis_index("dp")
    blocks, width = update.shape[0], lf.shape[2]
    tile = min(64, width)
    load = pltpu.make_async_copy(tab_v, tab, sems.at[0])
    load.start()

    def buffer_of(q):
        step = lax.rem(r - q + reps, reps)
        return jnp.where(step < 2, step, 5 - step)

    def mine(row):
        values = tab_v[row : row + 1, :]
        lane = lax.broadcasted_iota(jnp.int32, values.shape, 1)
        return jnp.sum(jnp.where(lane == d, values, 0))

    start, count = mine(ROW_START), mine(ROW_COUNT)
    weight = (1.0 - DECAY) / width
    sides = ((lf, left_gram, left_buf, left_out), (rf, right_gram, right_buf, right_out))
    for s in range(CAP):
        valid = s < count
        i = buffer_of((start + s) & 3)
        for factor, gram, buf, out in sides:
            for m in range(0, width, tile):
                sl = pl.ds(m, tile)
                buf[s, sl, :] = DECAY * factor[s, sl, :] + jnp.where(valid, weight * gram[i, sl, :], 0.0)
                pltpu.make_async_copy(buf.at[s, sl], out.at[s, sl], sems.at[2]).start()

    def put(b, carry):
        pos = tab[ROW_POS, b]
        pltpu.make_async_copy(uall.at[buffer_of(pos & 3), pos >> 2], update.at[b], sems.at[1]).start()
        return carry

    load.wait()
    lax.fori_loop(0, blocks, put, 0)
    pltpu.make_async_copy(left_buf, left_out, sems.at[2]).wait()
    pltpu.make_async_copy(right_buf, right_out, sems.at[2]).wait()
    pltpu.make_async_copy(uall, uall, sems.at[1]).wait()


def shards(reps, devs, gradient, owner, left_factor, right_factor, left_root, right_root):
    bf16, f32 = jnp.bfloat16, jnp.float32
    _, blocks, rows, width = gradient.shape
    places = blocks // reps
    part = width // CHUNKS
    any_spec = pl.BlockSpec(memory_space=pl.ANY)
    hbm_spec = pl.BlockSpec(memory_space=pltpu.HBM)
    vmem_spec = pl.BlockSpec(memory_space=pltpu.VMEM)
    dma = pltpu.SemaphoreType.DMA
    three = len(STEPS)
    tab, left_gram, right_gram, uall, lf, rf = pl.pallas_call(
        functools.partial(exchange, reps, devs),
        name="exchange",
        out_shape=[
            in_vmem((TAB_ROWS, 128), jnp.int32),
            in_vmem((CAP, width, width), f32),
            in_vmem((CAP, width, width), f32),
            in_vmem((CAP, places, rows, width), bf16),
            in_vmem((CAP, width, width), f32),
            in_vmem((CAP, width, width), f32),
        ],
        in_specs=[hbm_spec] * 6,
        out_specs=[vmem_spec] * 6,
        scratch_shapes=[
            pltpu.SMEM((TAB_ROWS, 128), jnp.int32),
            pltpu.VMEM((CAP, width, width), bf16),
            pltpu.VMEM((1, blocks), jnp.int32),
            pltpu.VMEM((blocks, rows, width), bf16),
            pltpu.VMEM((CAP, width, width), bf16),
            pltpu.VMEM((CAP, width, width), bf16),
            pltpu.VMEM((CHUNKS, PIECES, places // 2, rows, part), bf16),
            pltpu.VMEM((CHUNKS, PIECES, places // 2, rows, part), bf16),
            pltpu.VMEM((CAP, devs, rows, width), bf16),
            pltpu.VMEM((width, width), bf16),
            pltpu.VMEM((width, width), f32),
            pltpu.VMEM((width, width), bf16),
            [pltpu.VMEM((places, rows, part), bf16)] * CHUNKS,
            [pltpu.VMEM((places, rows, part), bf16)] * (CHUNKS * three),
            [pltpu.VMEM((devs, rows, (e - b) * width // BACK[-1]), bf16) for b, e in zip(BACK, BACK[1:])],
            dma((7,)),
            dma((CHUNKS, PIECES)),
            dma((CHUNKS, PIECES)),
            dma((CHUNKS, PIECES)),
            dma((CHUNKS, PIECES)),
            dma((CHUNKS,)),
            dma((CHUNKS,)),
            dma((CHUNKS, three)),
            dma((CHUNKS, three)),
            dma((CHUNKS, PIECES)),
            dma((CHUNKS, PIECES)),
            dma((len(BACK) - 1,)),
            dma((len(BACK) - 1,)),
            dma((len(BACK) - 1, PIECES)),
            dma((len(BACK) - 1, PIECES)),
        ],
        compiler_params=pltpu.CompilerParams(
            collective_id=0, has_side_effects=True, vmem_limit_bytes=40 * 2**20
        ),
    )(in_hbm(owner.reshape(1, blocks)), *(in_hbm(x) for x in (gradient, left_factor, right_factor, left_root, right_root)))
    update, left_out, right_out = pl.pallas_call(
        functools.partial(write_out, reps),
        name="write_out",
        out_shape=[
            jax.ShapeDtypeStruct((blocks, rows, width), bf16),
            jax.ShapeDtypeStruct((CAP, width, width), f32),
            jax.ShapeDtypeStruct((CAP, width, width), f32),
        ],
        in_specs=[vmem_spec] * 6,
        out_specs=[hbm_spec] * 3,
        scratch_shapes=[
            pltpu.SMEM((TAB_ROWS, 128), jnp.int32),
            pltpu.VMEM((CAP, width, width), f32),
            pltpu.VMEM((CAP, width, width), f32),
            dma((3,)),
        ],
        compiler_params=pltpu.CompilerParams(vmem_limit_bytes=24 * 2**20),
    )(*(from_vmem(x) for x in (tab, left_gram, right_gram, uall, lf, rf)))
    return update, left_out, right_out


def solution(mesh):
    in_specs = (
        P("rep", None, "dp", None),
        P(),
        P("dp", None, None),
        P("dp", None, None),
        P("dp", None, None),
        P("dp", None, None),
    )
    out_specs = (P(None, "dp", None), P("dp", None, None), P("dp", None, None))
    body = functools.partial(shards, mesh.shape["rep"], mesh.shape["dp"])
    return jax.shard_map(body, mesh=mesh, in_specs=in_specs, out_specs=out_specs, check_vma=False)
```

```python
import functools

import jax
import jax.numpy as jnp
from jax import lax
from jax.experimental import pallas as pl
from jax.experimental.pallas import tpu as pltpu
from jax.sharding import PartitionSpec as P

MESH = pl.DeviceIdType.MESH
CAP = 4
DECAY = 0.9
EPS = 1e-06
CHUNKS = 2
BACK = (0, 256, 512)
PIECES = 6
STEPS = (1, 3, 2)
TAB_ROWS = 16
ROW_BLOCK, ROW_POS, ROW_OWNER, ROW_START, ROW_COUNT, ROW_PLACE = 0, 1, 2, 3, 4, 5


def far_order():
    near = {0: 0, 1: 1, 2: 2, 3: 1}
    every = [(z, x, c) for z in range(4) for x in range(4) for c in range(2) if (z, x, c) != (0, 0, 0)]
    return sorted(every, key=lambda p: -(near[p[0]] + near[p[1]]))


def in_vmem(shape, dtype):
    return pltpu.VMEM(shape, dtype)


def in_hbm(x):
    return pltpu.with_memory_space_constraint(x, pltpu.HBM)


def from_vmem(x):
    return pltpu.with_memory_space_constraint(x, pltpu.VMEM)


def fill_tables(owner_ref, tab_ref):
    blocks = owner_ref.shape[1]
    lanes = tab_ref.shape[1]
    b = lax.broadcasted_iota(jnp.int32, (blocks, lanes), 0)
    c = lax.broadcasted_iota(jnp.int32, (blocks, lanes), 1)

    def down(x):
        return jnp.sum(x, axis=0, keepdims=True)

    inside = c < blocks
    row = jnp.broadcast_to(jnp.pad(owner_ref[...], ((0, 0), (0, lanes - blocks))), (blocks, lanes))
    col = jnp.sum(jnp.where(b == c, row, 0), axis=1, keepdims=True)
    col = jnp.broadcast_to(col, (blocks, lanes))
    before = (row < col) | ((row == col) & (c < b))
    pos_col = jnp.sum(jnp.where(before & inside, 1, 0), axis=1, keepdims=True)
    pos_col = jnp.broadcast_to(pos_col, (blocks, lanes))
    after = (col < row) | ((col == row) & (b < c))
    pos_row = down(jnp.where(after, 1, 0))
    here = pos_col == c
    start = down(jnp.where(col < c, 1, 0))
    count = down(jnp.where(col == c, 1, 0))
    tab_ref[ROW_BLOCK : ROW_BLOCK + 1, :] = down(jnp.where(here, b, 0))
    tab_ref[ROW_POS : ROW_POS + 1, :] = pos_row
    tab_ref[ROW_OWNER : ROW_OWNER + 1, :] = down(jnp.where(here, col, 0))
    tab_ref[ROW_START : ROW_START + 1, :] = start
    tab_ref[ROW_COUNT : ROW_COUNT + 1, :] = count
    for q in range(CAP):
        slot = (q - start) & 3
        place = jnp.where(slot < count, (start + slot) >> 2, 0)
        tab_ref[ROW_PLACE + q : ROW_PLACE + q + 1, :] = place
    rest = ROW_PLACE + CAP
    tab_ref[rest:, :] = jnp.zeros((TAB_ROWS - rest, lanes), jnp.int32)


def exchange(
    reps, devs, owner_hbm, grad_hbm, lf_hbm, rf_hbm, lr_hbm, rr_hbm,
    tab_out, left_gram, right_gram, uall, lf_out, rf_out,
    tab, gath, owner, grad, lroot, rroot, rs_send, rs_recv, stage, half, direct, upd, s_own, s_recv, back,
    loc_sem, rs_ss, rs_rs, ag_ss, ag_rs, pr_ss, pr_rs, ot_ss, ot_rs, ow_ss, ow_rs, bk_ss, bk_rs, au_ss, au_rs,
):
    r = lax.axis_index("rep")
    d = lax.axis_index("dp")
    places, rows, width = s_own[0].shape[0], grad.shape[1], grad.shape[2]
    part = width // CHUNKS
    cols = [pl.ds(c * part, part) for c in range(CHUNKS)]
    bcols = [pl.ds(b * width // BACK[-1], (e - b) * width // BACK[-1]) for b, e in zip(BACK, BACK[1:])]
    tile = min(256, width)
    mine = pl.ds(pl.multiple_of(d * rows, rows), rows)
    few = places // 2
    first, last = pl.ds(0, few), pl.ds(few, few)

    def rep_of(k):
        return lax.rem(r + k, reps)

    def dp_peer(t):
        if not isinstance(t, tuple):
            return lax.rem(d + t, devs)
        dz, dx, dc = t
        z, x, c = d // 8, lax.rem(d // 2, 4), lax.rem(d, 2)
        return lax.rem(z + dz, 4) * 8 + lax.rem(x + dx, 4) * 2 + lax.rem(c + dc, 2)

    def local(src, dst, i):
        return pltpu.make_async_copy(src, dst, loc_sem.at[i])

    load_owner, load_grad = local(owner_hbm, owner, 0), local(grad_hbm.at[0], grad, 1)
    load_roots = [local(lr_hbm, lroot, 2), local(rr_hbm, rroot, 3)]
    load_factors = [local(lf_hbm, lf_out, 4), local(rf_hbm, rf_out, 5)]
    load_owner.start()
    load_grad.start()

    barrier = pltpu.get_barrier_semaphore()
    for k in STEPS:
        pl.semaphore_signal(barrier, inc=1, device_id=(rep_of(k), d), device_id_type=MESH)

    def greet(t, carry):
        pl.semaphore_signal(barrier, inc=1, device_id=(r, dp_peer(t)), device_id_type=MESH)
        return carry

    for p in far_order():
        greet(p, 0)

    load_owner.wait()
    fill_tables(owner, tab_out)
    to_scalars = local(tab_out, tab, 6)
    to_scalars.start()
    to_scalars.wait()
    load_grad.wait()

    def to_rep(piece, src, dst, ss, rs):
        copy = pltpu.make_async_remote_copy(
            src_ref=src,
            dst_ref=dst,
            send_sem=ss.at[piece],
            recv_sem=rs.at[piece],
            device_id=(rep_of(1 if piece % 2 == 0 else reps - 1), d),
            device_id_type=MESH,
        )
        copy.start()
        return copy

    packing = ((2, 0), (2, few), (1, few), (reps - 1, 0), (1, 0), (reps - 1, few))

    def pack(pieces, c):
        def step(j, carry):
            for p in pieces:
                k, at = packing[p]
                block = tab[ROW_BLOCK, CAP * (at + j) + rep_of(k)]
                rows_here = grad[block, :, cols[c]]
                if p >= 4:
                    both = rows_here.astype(jnp.float32) + rs_recv[c, p - 4, j].astype(jnp.float32)
                    rows_here = both.astype(jnp.bfloat16)
                rs_send[c, p, j] = rows_here
            return carry

        lax.fori_loop(0, few, step, 0, unroll=True)

    def send_sums(p, c):
        return to_rep(p, rs_send.at[c, p], rs_recv.at[c, p], rs_ss.at[c], rs_rs.at[c])

    for c in range(CHUNKS):
        pack((0, 1, 2, 3), c)
    pl.semaphore_wait(barrier, reps - 1 + devs - 1)
    rs = [{p: send_sums(p, c) for p in (range(4) if c == 0 else range(2))} for c in range(CHUNKS)]
    for load in load_roots + load_factors:
        load.start()
    for c in range(CHUNKS):
        for p in (4, 5):
            rs[c][p - 4].wait_recv()
            pack((p,), c)
            rs[c][p] = send_sums(p, c)
        if c == 0:
            for e in range(1, CHUNKS):
                for p in (2, 3):
                    rs[e][p] = send_sums(p, e)

    def share(pieces, buf, ss, rs):
        halves = (first, last, last, first)
        return {p: to_rep(p, buf(0, halves[p]), buf(1 + p % 2, halves[p]), ss, rs) for p in pieces}

    def pass_on(copies, buf, ss, rs):
        copies[0].wait_recv()
        copies[4] = to_rep(4, buf(1, first), buf(3, first), ss, rs)
        copies[1].wait_recv()
        copies[5] = to_rep(5, buf(2, last), buf(3, last), ss, rs)

    def sums(c):
        return lambda i, sl: (s_own[c] if i == 0 else s_recv[(i - 1) * CHUNKS + c]).at[sl]

    def one(src, dst, ss, rs, to):
        pltpu.make_async_remote_copy(
            src_ref=src, dst_ref=dst, send_sem=ss, recv_sem=rs, device_id=(r, to), device_id_type=MESH
        ).start()

    def to_owners(i, c, q, src, ss, rs):
        def step(t, carry):
            o = dp_peer(t)
            stage[i, o, :, cols[c]] = src[tab[ROW_PLACE + q, o]]
            one(stage.at[i, o, :, cols[c]], gath.at[i, mine, cols[c]], ss, rs, o)
            return carry

        for p in far_order():
            step(p, 0)
        gath[i, mine, cols[c]] = src[tab[ROW_PLACE + q, d]]

    ag = []
    for c in range(CHUNKS):
        for p in (2, 3, 4, 5):
            rs[c][p].wait_recv()

        def add(j, carry, c=c):
            for at, pieces in ((0, (4, 3)), (few, (2, 5))):
                total = grad[tab[ROW_BLOCK, CAP * (at + j) + r], :, cols[c]].astype(jnp.float32)
                for p in pieces:
                    total += rs_recv[c, p, j].astype(jnp.float32)
                s_own[c][at + j] = total.astype(jnp.bfloat16)
            return carry

        lax.fori_loop(0, few, add, 0, unroll=True)
        ag.append(share((0, 1, 2 + c % 2), sums(c), ag_ss.at[c], ag_rs.at[c]) if c == 0 else {})
        to_owners(0, c, r, s_own[c], pr_ss.at[c], pr_rs.at[c])
        if c > 0:
            ag[c] = share((0, 1, 2 + c % 2), sums(c), ag_ss.at[c], ag_rs.at[c])

    def pass_sums_on(c):
        pass_on(ag[c], sums(c), ag_ss.at[c], ag_rs.at[c])

    def others(i, c):
        for p in ((2,), (3,), (4, 5))[i - 1]:
            ag[c][p].wait_recv()
        q = rep_of(reps - STEPS[i - 1])
        to_owners(i, c, q, s_recv[(i - 1) * CHUNKS + c], ot_ss.at[c, i - 1], ot_rs.at[c, i - 1])

    def from_neighbour(i, c):
        arrived = gath.at[0, :, cols[c]]
        return to_rep(i, arrived, gath.at[1 + i, :, cols[c]], ow_ss.at[c], ow_rs.at[c])

    pass_sums_on(0)
    others(1, 0)
    for c in range(1, CHUNKS):
        pass_sums_on(c)

    slot = (r - tab[ROW_START, d]) & 3
    for load in load_roots:
        load.wait()
    ow = []
    for c in range(CHUNKS):
        arrived = gath.at[0, pl.ds(0, rows * (devs - 1)), cols[c]]
        pltpu.make_async_copy(arrived, arrived, pr_rs.at[c]).wait()
        ow.append(from_neighbour(1 - c % 2, c))
        for m in range(0, width, tile):
            half[m : m + tile, cols[c]] = jnp.dot(
                lroot[slot, m : m + tile, :], gath[0, :, cols[c]], preferred_element_type=jnp.float32
            ).astype(jnp.bfloat16)
    grad_sq = jnp.zeros((1, 1), jnp.float32)
    dir_sq = jnp.zeros((1, 1), jnp.float32)
    for m in range(0, width, tile):
        piece = jnp.dot(half[m : m + tile, :], rroot[slot], preferred_element_type=jnp.float32)
        direct[m : m + tile, :] = piece
        dir_sq += jnp.sum(piece * piece, keepdims=True)
        g = gath[0, m : m + tile, :].astype(jnp.float32)
        grad_sq += jnp.sum(g * g, keepdims=True)
    scale = jnp.sqrt(grad_sq) / jnp.sqrt(dir_sq + EPS)
    for m in range(0, width, tile):
        upd[m : m + tile, :] = (direct[m : m + tile, :] * scale).astype(jnp.bfloat16)

    for c in range(len(bcols)):

        def homeward(t, carry, c=c):
            to = dp_peer(t)
            theirs = pl.ds(pl.multiple_of(to * rows, rows), rows)
            one(upd.at[theirs, bcols[c]], back[c].at[d], bk_ss.at[c], bk_rs.at[c], to)
            return carry

        for p in far_order():
            homeward(p, 0)
        back[c][d] = upd[mine, bcols[c]]

    for c in range(1, CHUNKS):
        others(1 + c % 2, c)
    for c in range(CHUNKS):
        for p in (4, 5):
            ag[c][p].wait_recv()
    far = rep_of(reps - STEPS[2])

    def to_far_owner(t, carry):
        o = dp_peer(t)
        place = tab[ROW_PLACE + far, o]
        for c in range(CHUNKS):
            stage[3, o, :, cols[c]] = s_recv[2 * CHUNKS + c][place]
        one(stage.at[3, o], gath.at[3, mine, :], ot_ss.at[0, 2], ot_rs.at[0, 2], o)
        return carry

    for p in far_order():
        to_far_owner(p, 0)
    for c in range(CHUNKS):
        gath[3, mine, cols[c]] = s_recv[2 * CHUNKS + c][tab[ROW_PLACE + far, d]]

    def gram(i):
        if i == 3:
            arrived = gath.at[3, pl.ds(0, rows * (devs - 1)), :]
            pltpu.make_async_copy(arrived, arrived, ot_rs.at[0, 2]).wait()
        elif i > 0:
            for c in range(CHUNKS):
                if i == 1 + c % 2:
                    arrived = gath.at[i, pl.ds(0, rows * (devs - 1)), cols[c]]
                    pltpu.make_async_copy(arrived, arrived, ot_rs.at[c, i - 1]).wait()
                else:
                    ow[c].wait_recv()
        for m in range(0, width, tile):
            sl = pl.ds(m, tile)
            left_gram[i, sl, :] = lax.dot_general(
                gath[i, sl, :], gath[i], (((1,), (1,)), ((), ())), preferred_element_type=jnp.float32
            )
            right_gram[i, sl, :] = lax.dot_general(
                gath[i, :, sl], gath[i], (((0,), (0,)), ((), ())), preferred_element_type=jnp.float32
            )

    gram(0)

    gram(1)

    def steps(c):
        return lambda i, sl: uall.at[i, sl, :, bcols[c]]

    au = []
    for c in range(len(bcols)):
        arrived = back[c].at[pl.ds(0, devs - 1)]
        pltpu.make_async_copy(arrived, arrived, bk_rs.at[c]).wait()

        def unpack(j, carry, c=c):
            uall[0, j, :, bcols[c]] = back[c][tab[ROW_OWNER, CAP * j + r]]
            return carry

        lax.fori_loop(0, places, unpack, 0, unroll=True)
        au.append(share((0, 1), steps(c), au_ss.at[c], au_rs.at[c]))
        if c > 0:
            pass_on(au[c - 1], steps(c - 1), au_ss.at[c - 1], au_rs.at[c - 1])
        au[c].update(share((2, 3), steps(c), au_ss.at[c], au_rs.at[c]))
    pass_on(au[-1], steps(len(bcols) - 1), au_ss.at[len(bcols) - 1], au_rs.at[len(bcols) - 1])
    gram(2)
    gram(3)

    for c in range(CHUNKS):
        for copy in list(rs[c].values()) + list(ag[c].values()) + [ow[c]]:
            copy.wait_send()
        for i in (0, 1 + c % 2):
            sent = stage.at[i, pl.ds(0, devs - 1), :, cols[c]]
            pltpu.make_async_copy(sent, sent, pr_ss.at[c] if i == 0 else ot_ss.at[c, i - 1]).wait()
    sent = stage.at[3, pl.ds(0, devs - 1)]
    pltpu.make_async_copy(sent, sent, ot_ss.at[0, 2]).wait()
    for c in range(len(bcols)):
        for copy in au[c].values():
            copy.wait_send()
        sent = back[c].at[pl.ds(0, devs - 1)]
        pltpu.make_async_copy(sent, sent, bk_ss.at[c]).wait()
        for p in (2, 3, 4, 5):
            au[c][p].wait_recv()
    for load in load_factors:
        load.wait()


def write_out(
    reps, tab_v, left_gram, right_gram, uall, lf, rf, update, left_out, right_out, tab, left_buf, right_buf, sems
):
    r = lax.axis_index("rep")
    d = lax.axis_index("dp")
    blocks, width = update.shape[0], lf.shape[2]
    tile = min(64, width)
    load = pltpu.make_async_copy(tab_v, tab, sems.at[0])
    load.start()

    def buffer_of(q):
        step = lax.rem(r - q + reps, reps)
        return jnp.where(step < 2, step, 5 - step)

    def mine(row):
        values = tab_v[row : row + 1, :]
        lane = lax.broadcasted_iota(jnp.int32, values.shape, 1)
        return jnp.sum(jnp.where(lane == d, values, 0))

    start, count = mine(ROW_START), mine(ROW_COUNT)
    weight = (1.0 - DECAY) / width
    sides = ((lf, left_gram, left_buf, left_out), (rf, right_gram, right_buf, right_out))
    for s in range(CAP):
        valid = s < count
        i = buffer_of((start + s) & 3)
        for factor, gram, buf, out in sides:
            for m in range(0, width, tile):
                sl = pl.ds(m, tile)
                buf[s, sl, :] = DECAY * factor[s, sl, :] + jnp.where(valid, weight * gram[i, sl, :], 0.0)
                pltpu.make_async_copy(buf.at[s, sl], out.at[s, sl], sems.at[2]).start()

    def put(b, carry):
        pos = tab[ROW_POS, b]
        pltpu.make_async_copy(uall.at[buffer_of(pos & 3), pos >> 2], update.at[b], sems.at[1]).start()
        return carry

    load.wait()
    lax.fori_loop(0, blocks, put, 0)
    pltpu.make_async_copy(left_buf, left_out, sems.at[2]).wait()
    pltpu.make_async_copy(right_buf, right_out, sems.at[2]).wait()
    pltpu.make_async_copy(uall, uall, sems.at[1]).wait()


def shards(reps, devs, gradient, owner, left_factor, right_factor, left_root, right_root):
    bf16, f32 = jnp.bfloat16, jnp.float32
    _, blocks, rows, width = gradient.shape
    places = blocks // reps
    part = width // CHUNKS
    any_spec = pl.BlockSpec(memory_space=pl.ANY)
    hbm_spec = pl.BlockSpec(memory_space=pltpu.HBM)
    vmem_spec = pl.BlockSpec(memory_space=pltpu.VMEM)
    dma = pltpu.SemaphoreType.DMA
    three = len(STEPS)
    tab, left_gram, right_gram, uall, lf, rf = pl.pallas_call(
        functools.partial(exchange, reps, devs),
        name="exchange",
        out_shape=[
            in_vmem((TAB_ROWS, 128), jnp.int32),
            in_vmem((CAP, width, width), f32),
            in_vmem((CAP, width, width), f32),
            in_vmem((CAP, places, rows, width), bf16),
            in_vmem((CAP, width, width), f32),
            in_vmem((CAP, width, width), f32),
        ],
        in_specs=[hbm_spec] * 6,
        out_specs=[vmem_spec] * 6,
        scratch_shapes=[
            pltpu.SMEM((TAB_ROWS, 128), jnp.int32),
            pltpu.VMEM((CAP, width, width), bf16),
            pltpu.VMEM((1, blocks), jnp.int32),
            pltpu.VMEM((blocks, rows, width), bf16),
            pltpu.VMEM((CAP, width, width), bf16),
            pltpu.VMEM((CAP, width, width), bf16),
            pltpu.VMEM((CHUNKS, PIECES, places // 2, rows, part), bf16),
            pltpu.VMEM((CHUNKS, PIECES, places // 2, rows, part), bf16),
            pltpu.VMEM((CAP, devs, rows, width), bf16),
            pltpu.VMEM((width, width), bf16),
            pltpu.VMEM((width, width), f32),
            pltpu.VMEM((width, width), bf16),
            [pltpu.VMEM((places, rows, part), bf16)] * CHUNKS,
            [pltpu.VMEM((places, rows, part), bf16)] * (CHUNKS * three),
            [pltpu.VMEM((devs, rows, (e - b) * width // BACK[-1]), bf16) for b, e in zip(BACK, BACK[1:])],
            dma((7,)),
            dma((CHUNKS, PIECES)),
            dma((CHUNKS, PIECES)),
            dma((CHUNKS, PIECES)),
            dma((CHUNKS, PIECES)),
            dma((CHUNKS,)),
            dma((CHUNKS,)),
            dma((CHUNKS, three)),
            dma((CHUNKS, three)),
            dma((CHUNKS, PIECES)),
            dma((CHUNKS, PIECES)),
            dma((len(BACK) - 1,)),
            dma((len(BACK) - 1,)),
            dma((len(BACK) - 1, PIECES)),
            dma((len(BACK) - 1, PIECES)),
        ],
        compiler_params=pltpu.CompilerParams(
            collective_id=0, has_side_effects=True, vmem_limit_bytes=40 * 2**20
        ),
    )(in_hbm(owner.reshape(1, blocks)), *(in_hbm(x) for x in (gradient, left_factor, right_factor, left_root, right_root)))
    update, left_out, right_out = pl.pallas_call(
        functools.partial(write_out, reps),
        name="write_out",
        out_shape=[
            jax.ShapeDtypeStruct((blocks, rows, width), bf16),
            jax.ShapeDtypeStruct((CAP, width, width), f32),
            jax.ShapeDtypeStruct((CAP, width, width), f32),
        ],
        in_specs=[vmem_spec] * 6,
        out_specs=[hbm_spec] * 3,
        scratch_shapes=[
            pltpu.SMEM((TAB_ROWS, 128), jnp.int32),
            pltpu.VMEM((CAP, width, width), f32),
            pltpu.VMEM((CAP, width, width), f32),
            dma((3,)),
        ],
        compiler_params=pltpu.CompilerParams(vmem_limit_bytes=24 * 2**20),
    )(*(from_vmem(x) for x in (tab, left_gram, right_gram, uall, lf, rf)))
    return update, left_out, right_out


def solution(mesh):
    in_specs = (
        P("rep", None, "dp", None),
        P(),
        P("dp", None, None),
        P("dp", None, None),
        P("dp", None, None),
        P("dp", None, None),
    )
    out_specs = (P(None, "dp", None), P("dp", None, None), P("dp", None, None))
    body = functools.partial(shards, mesh.shape["rep"], mesh.shape["dp"])
    return jax.shard_map(body, mesh=mesh, in_specs=in_specs, out_specs=out_specs, check_vma=False)
```

```python
import functools

import jax
import jax.numpy as jnp
from jax import lax
from jax.experimental import pallas as pl
from jax.experimental.pallas import tpu as pltpu
from jax.sharding import PartitionSpec as P

MESH = pl.DeviceIdType.MESH
CAP = 4
DECAY = 0.9
EPS = 1e-06
CHUNKS = 2
BACK = (0, 256, 512)
PIECES = 6
STEPS = (1, 3, 2)
TAB_ROWS = 16
ROW_BLOCK, ROW_POS, ROW_OWNER, ROW_START, ROW_COUNT, ROW_PLACE = 0, 1, 2, 3, 4, 5


def far_order():
    near = {0: 0, 1: 1, 2: 2, 3: 1}
    every = [(z, x, c) for z in range(4) for x in range(4) for c in range(2) if (z, x, c) != (0, 0, 0)]
    return sorted(every, key=lambda p: -(near[p[0]] + near[p[1]]))


def in_vmem(shape, dtype):
    return pltpu.VMEM(shape, dtype)


def in_hbm(x):
    return pltpu.with_memory_space_constraint(x, pltpu.HBM)


def from_vmem(x):
    return pltpu.with_memory_space_constraint(x, pltpu.VMEM)


def fill_tables(owner_ref, tab_ref):
    blocks = owner_ref.shape[1]
    lanes = tab_ref.shape[1]
    b = lax.broadcasted_iota(jnp.int32, (blocks, lanes), 0)
    c = lax.broadcasted_iota(jnp.int32, (blocks, lanes), 1)

    def down(x):
        return jnp.sum(x, axis=0, keepdims=True)

    inside = c < blocks
    row = jnp.broadcast_to(jnp.pad(owner_ref[...], ((0, 0), (0, lanes - blocks))), (blocks, lanes))
    col = jnp.sum(jnp.where(b == c, row, 0), axis=1, keepdims=True)
    col = jnp.broadcast_to(col, (blocks, lanes))
    before = (row < col) | ((row == col) & (c < b))
    pos_col = jnp.sum(jnp.where(before & inside, 1, 0), axis=1, keepdims=True)
    pos_col = jnp.broadcast_to(pos_col, (blocks, lanes))
    after = (col < row) | ((col == row) & (b < c))
    pos_row = down(jnp.where(after, 1, 0))
    here = pos_col == c
    start = down(jnp.where(col < c, 1, 0))
    count = down(jnp.where(col == c, 1, 0))
    tab_ref[ROW_BLOCK : ROW_BLOCK + 1, :] = down(jnp.where(here, b, 0))
    tab_ref[ROW_POS : ROW_POS + 1, :] = pos_row
    tab_ref[ROW_OWNER : ROW_OWNER + 1, :] = down(jnp.where(here, col, 0))
    tab_ref[ROW_START : ROW_START + 1, :] = start
    tab_ref[ROW_COUNT : ROW_COUNT + 1, :] = count
    for q in range(CAP):
        slot = (q - start) & 3
        place = jnp.where(slot < count, (start + slot) >> 2, 0)
        tab_ref[ROW_PLACE + q : ROW_PLACE + q + 1, :] = place
    rest = ROW_PLACE + CAP
    tab_ref[rest:, :] = jnp.zeros((TAB_ROWS - rest, lanes), jnp.int32)


def exchange(
    reps, devs, owner_hbm, grad_hbm, lf_hbm, rf_hbm, lr_hbm, rr_hbm,
    tab_out, left_gram, right_gram, uall, lf_out, rf_out,
    tab, gath, owner, grad, lroot, rroot, rs_send, rs_recv, stage, half, direct, upd, s_own, s_recv, back,
    loc_sem, rs_ss, rs_rs, ag_ss, ag_rs, pr_ss, pr_rs, ot_ss, ot_rs, ow_ss, ow_rs, bk_ss, bk_rs, au_ss, au_rs,
):
    r = lax.axis_index("rep")
    d = lax.axis_index("dp")
    places, rows, width = s_own[0].shape[0], grad.shape[1], grad.shape[2]
    part = width // CHUNKS
    cols = [pl.ds(c * part, part) for c in range(CHUNKS)]
    bcols = [pl.ds(b * width // BACK[-1], (e - b) * width // BACK[-1]) for b, e in zip(BACK, BACK[1:])]
    tile = min(256, width)
    mine = pl.ds(pl.multiple_of(d * rows, rows), rows)
    few = places // 2
    first, last = pl.ds(0, few), pl.ds(few, few)

    def rep_of(k):
        return lax.rem(r + k, reps)

    def dp_peer(t):
        if not isinstance(t, tuple):
            return lax.rem(d + t, devs)
        dz, dx, dc = t
        z, x, c = d // 8, lax.rem(d // 2, 4), lax.rem(d, 2)
        return lax.rem(z + dz, 4) * 8 + lax.rem(x + dx, 4) * 2 + lax.rem(c + dc, 2)

    def local(src, dst, i):
        return pltpu.make_async_copy(src, dst, loc_sem.at[i])

    load_owner, load_grad = local(owner_hbm, owner, 0), local(grad_hbm.at[0], grad, 1)
    load_roots = [local(lr_hbm, lroot, 2), local(rr_hbm, rroot, 3)]
    load_factors = [local(lf_hbm, lf_out, 4), local(rf_hbm, rf_out, 5)]
    load_owner.start()
    load_grad.start()

    barrier = pltpu.get_barrier_semaphore()
    for k in STEPS:
        pl.semaphore_signal(barrier, inc=1, device_id=(rep_of(k), d), device_id_type=MESH)

    def greet(t, carry):
        pl.semaphore_signal(barrier, inc=1, device_id=(r, dp_peer(t)), device_id_type=MESH)
        return carry

    for p in far_order():
        greet(p, 0)

    load_owner.wait()
    fill_tables(owner, tab_out)
    to_scalars = local(tab_out, tab, 6)
    to_scalars.start()
    to_scalars.wait()
    load_grad.wait()

    def to_rep(piece, src, dst, ss, rs):
        copy = pltpu.make_async_remote_copy(
            src_ref=src,
            dst_ref=dst,
            send_sem=ss.at[piece],
            recv_sem=rs.at[piece],
            device_id=(rep_of(1 if piece % 2 == 0 else reps - 1), d),
            device_id_type=MESH,
        )
        copy.start()
        return copy

    packing = ((2, 0), (2, few), (1, few), (reps - 1, 0), (1, 0), (reps - 1, few))

    def pack(pieces, c):
        def step(j, carry):
            for p in pieces:
                k, at = packing[p]
                block = tab[ROW_BLOCK, CAP * (at + j) + rep_of(k)]
                rows_here = grad[block, :, cols[c]]
                if p >= 4:
                    both = rows_here.astype(jnp.float32) + rs_recv[c, p - 4, j].astype(jnp.float32)
                    rows_here = both.astype(jnp.bfloat16)
                rs_send[c, p, j] = rows_here
            return carry

        lax.fori_loop(0, few, step, 0, unroll=True)

    def send_sums(p, c):
        return to_rep(p, rs_send.at[c, p], rs_recv.at[c, p], rs_ss.at[c], rs_rs.at[c])

    for c in range(CHUNKS):
        pack((0, 1, 2, 3), c)
    pl.semaphore_wait(barrier, reps - 1 + devs - 1)
    rs = [{p: send_sums(p, c) for p in (range(4) if c == 0 else range(2))} for c in range(CHUNKS)]
    for load in load_roots + load_factors:
        load.start()
    for c in range(CHUNKS):
        for p in (4, 5):
            rs[c][p - 4].wait_recv()
            pack((p,), c)
            rs[c][p] = send_sums(p, c)
        if c == 0:
            for e in range(1, CHUNKS):
                for p in (2, 3):
                    rs[e][p] = send_sums(p, e)

    def share(pieces, buf, ss, rs):
        halves = (first, last, last, first)
        return {p: to_rep(p, buf(0, halves[p]), buf(1 + p % 2, halves[p]), ss, rs) for p in pieces}

    def pass_on(copies, buf, ss, rs):
        copies[0].wait_recv()
        copies[4] = to_rep(4, buf(1, first), buf(3, first), ss, rs)
        copies[1].wait_recv()
        copies[5] = to_rep(5, buf(2, last), buf(3, last), ss, rs)

    def sums(c):
        return lambda i, sl: (s_own[c] if i == 0 else s_recv[(i - 1) * CHUNKS + c]).at[sl]

    def one(src, dst, ss, rs, to):
        pltpu.make_async_remote_copy(
            src_ref=src, dst_ref=dst, send_sem=ss, recv_sem=rs, device_id=(r, to), device_id_type=MESH
        ).start()

    def to_owners(i, c, q, src, ss, rs):
        def step(t, carry):
            o = dp_peer(t)
            stage[i, o, :, cols[c]] = src[tab[ROW_PLACE + q, o]]
            one(stage.at[i, o, :, cols[c]], gath.at[i, mine, cols[c]], ss, rs, o)
            return carry

        for p in far_order():
            step(p, 0)
        gath[i, mine, cols[c]] = src[tab[ROW_PLACE + q, d]]

    ag = []
    for c in range(CHUNKS):
        for p in (2, 3, 4, 5):
            rs[c][p].wait_recv()

        def add(j, carry, c=c):
            for at, pieces in ((0, (4, 3)), (few, (2, 5))):
                total = grad[tab[ROW_BLOCK, CAP * (at + j) + r], :, cols[c]].astype(jnp.float32)
                for p in pieces:
                    total += rs_recv[c, p, j].astype(jnp.float32)
                s_own[c][at + j] = total.astype(jnp.bfloat16)
            return carry

        lax.fori_loop(0, few, add, 0, unroll=True)
        ag.append(share((0, 1, 2 + c % 2), sums(c), ag_ss.at[c], ag_rs.at[c]) if c == 0 else {})
        to_owners(0, c, r, s_own[c], pr_ss.at[c], pr_rs.at[c])
        if c > 0:
            ag[c] = share((0, 1, 2 + c % 2), sums(c), ag_ss.at[c], ag_rs.at[c])

    def pass_sums_on(c):
        pass_on(ag[c], sums(c), ag_ss.at[c], ag_rs.at[c])

    def others(i, c):
        for p in ((2,), (3,), (4, 5))[i - 1]:
            ag[c][p].wait_recv()
        q = rep_of(reps - STEPS[i - 1])
        to_owners(i, c, q, s_recv[(i - 1) * CHUNKS + c], ot_ss.at[c, i - 1], ot_rs.at[c, i - 1])

    def from_neighbour(i, c):
        arrived = gath.at[0, :, cols[c]]
        return to_rep(i, arrived, gath.at[1 + i, :, cols[c]], ow_ss.at[c], ow_rs.at[c])

    pass_sums_on(0)
    others(1, 0)
    for c in range(1, CHUNKS):
        pass_sums_on(c)

    slot = (r - tab[ROW_START, d]) & 3
    for load in load_roots:
        load.wait()
    ow = []
    for c in range(CHUNKS):
        arrived = gath.at[0, pl.ds(0, rows * (devs - 1)), cols[c]]
        pltpu.make_async_copy(arrived, arrived, pr_rs.at[c]).wait()
        ow.append(from_neighbour(1 - c % 2, c))
        for m in range(0, width, tile):
            half[m : m + tile, cols[c]] = jnp.dot(
                lroot[slot, m : m + tile, :], gath[0, :, cols[c]], preferred_element_type=jnp.float32
            ).astype(jnp.bfloat16)
    grad_sq = jnp.zeros((1, 1), jnp.float32)
    dir_sq = jnp.zeros((1, 1), jnp.float32)
    for m in range(0, width, tile):
        piece = jnp.dot(half[m : m + tile, :], rroot[slot], preferred_element_type=jnp.float32)
        direct[m : m + tile, :] = piece
        dir_sq += jnp.sum(piece * piece, keepdims=True)
        g = gath[0, m : m + tile, :].astype(jnp.float32)
        grad_sq += jnp.sum(g * g, keepdims=True)
    scale = jnp.sqrt(grad_sq) / jnp.sqrt(dir_sq + EPS)
    for m in range(0, width, tile):
        upd[m : m + tile, :] = (direct[m : m + tile, :] * scale).astype(jnp.bfloat16)

    for c in range(len(bcols)):

        def homeward(t, carry, c=c):
            to = dp_peer(t)
            theirs = pl.ds(pl.multiple_of(to * rows, rows), rows)
            one(upd.at[theirs, bcols[c]], back[c].at[d], bk_ss.at[c], bk_rs.at[c], to)
            return carry

        for p in far_order():
            homeward(p, 0)
        back[c][d] = upd[mine, bcols[c]]

    for c in range(1, CHUNKS):
        others(1 + c % 2, c)
    for c in range(CHUNKS):
        for p in (4, 5):
            ag[c][p].wait_recv()
    far = rep_of(reps - STEPS[2])

    def to_far_owner(t, carry):
        o = dp_peer(t)
        place = tab[ROW_PLACE + far, o]
        for c in range(CHUNKS):
            stage[3, o, :, cols[c]] = s_recv[2 * CHUNKS + c][place]
        one(stage.at[3, o], gath.at[3, mine, :], ot_ss.at[0, 2], ot_rs.at[0, 2], o)
        return carry

    for p in far_order():
        to_far_owner(p, 0)
    for c in range(CHUNKS):
        gath[3, mine, cols[c]] = s_recv[2 * CHUNKS + c][tab[ROW_PLACE + far, d]]

    def gram(i):
        if i == 3:
            arrived = gath.at[3, pl.ds(0, rows * (devs - 1)), :]
            pltpu.make_async_copy(arrived, arrived, ot_rs.at[0, 2]).wait()
        elif i > 0:
            for c in range(CHUNKS):
                if i == 1 + c % 2:
                    arrived = gath.at[i, pl.ds(0, rows * (devs - 1)), cols[c]]
                    pltpu.make_async_copy(arrived, arrived, ot_rs.at[c, i - 1]).wait()
                else:
                    ow[c].wait_recv()
        for m in range(0, width, tile):
            sl = pl.ds(m, tile)
            left_gram[i, sl, :] = lax.dot_general(
                gath[i, sl, :], gath[i], (((1,), (1,)), ((), ())), preferred_element_type=jnp.float32
            )
            right_gram[i, sl, :] = lax.dot_general(
                gath[i, :, sl], gath[i], (((0,), (0,)), ((), ())), preferred_element_type=jnp.float32
            )

    gram(0)

    gram(1)

    def steps(c):
        return lambda i, sl: uall.at[i, sl, :, bcols[c]]

    au = []
    for c in range(len(bcols)):
        arrived = back[c].at[pl.ds(0, devs - 1)]
        pltpu.make_async_copy(arrived, arrived, bk_rs.at[c]).wait()

        def unpack(j, carry, c=c):
            uall[0, j, :, bcols[c]] = back[c][tab[ROW_OWNER, CAP * j + r]]
            return carry

        lax.fori_loop(0, places, unpack, 0, unroll=True)
        au.append(share((0, 1), steps(c), au_ss.at[c], au_rs.at[c]))
        if c > 0:
            pass_on(au[c - 1], steps(c - 1), au_ss.at[c - 1], au_rs.at[c - 1])
        au[c].update(share((2, 3), steps(c), au_ss.at[c], au_rs.at[c]))
    gram(2)
    pass_on(au[-1], steps(len(bcols) - 1), au_ss.at[len(bcols) - 1], au_rs.at[len(bcols) - 1])
    gram(3)

    for c in range(CHUNKS):
        for copy in list(rs[c].values()) + list(ag[c].values()) + [ow[c]]:
            copy.wait_send()
        for i in (0, 1 + c % 2):
            sent = stage.at[i, pl.ds(0, devs - 1), :, cols[c]]
            pltpu.make_async_copy(sent, sent, pr_ss.at[c] if i == 0 else ot_ss.at[c, i - 1]).wait()
    sent = stage.at[3, pl.ds(0, devs - 1)]
    pltpu.make_async_copy(sent, sent, ot_ss.at[0, 2]).wait()
    for c in range(len(bcols)):
        for copy in au[c].values():
            copy.wait_send()
        sent = back[c].at[pl.ds(0, devs - 1)]
        pltpu.make_async_copy(sent, sent, bk_ss.at[c]).wait()
        for p in (2, 3, 4, 5):
            au[c][p].wait_recv()
    for load in load_factors:
        load.wait()


def write_out(
    reps, tab_v, left_gram, right_gram, uall, lf, rf, update, left_out, right_out, tab, left_buf, right_buf, sems
):
    r = lax.axis_index("rep")
    d = lax.axis_index("dp")
    blocks, width = update.shape[0], lf.shape[2]
    tile = min(64, width)
    load = pltpu.make_async_copy(tab_v, tab, sems.at[0])
    load.start()

    def buffer_of(q):
        step = lax.rem(r - q + reps, reps)
        return jnp.where(step < 2, step, 5 - step)

    def mine(row):
        values = tab_v[row : row + 1, :]
        lane = lax.broadcasted_iota(jnp.int32, values.shape, 1)
        return jnp.sum(jnp.where(lane == d, values, 0))

    start, count = mine(ROW_START), mine(ROW_COUNT)
    weight = (1.0 - DECAY) / width
    sides = ((lf, left_gram, left_buf, left_out), (rf, right_gram, right_buf, right_out))
    for s in range(CAP):
        valid = s < count
        i = buffer_of((start + s) & 3)
        for factor, gram, buf, out in sides:
            for m in range(0, width, tile):
                sl = pl.ds(m, tile)
                buf[s, sl, :] = DECAY * factor[s, sl, :] + jnp.where(valid, weight * gram[i, sl, :], 0.0)
                pltpu.make_async_copy(buf.at[s, sl], out.at[s, sl], sems.at[2]).start()

    def put(b, carry):
        pos = tab[ROW_POS, b]
        pltpu.make_async_copy(uall.at[buffer_of(pos & 3), pos >> 2], update.at[b], sems.at[1]).start()
        return carry

    load.wait()
    lax.fori_loop(0, blocks, put, 0)
    pltpu.make_async_copy(left_buf, left_out, sems.at[2]).wait()
    pltpu.make_async_copy(right_buf, right_out, sems.at[2]).wait()
    pltpu.make_async_copy(uall, uall, sems.at[1]).wait()


def shards(reps, devs, gradient, owner, left_factor, right_factor, left_root, right_root):
    bf16, f32 = jnp.bfloat16, jnp.float32
    _, blocks, rows, width = gradient.shape
    places = blocks // reps
    part = width // CHUNKS
    any_spec = pl.BlockSpec(memory_space=pl.ANY)
    hbm_spec = pl.BlockSpec(memory_space=pltpu.HBM)
    vmem_spec = pl.BlockSpec(memory_space=pltpu.VMEM)
    dma = pltpu.SemaphoreType.DMA
    three = len(STEPS)
    tab, left_gram, right_gram, uall, lf, rf = pl.pallas_call(
        functools.partial(exchange, reps, devs),
        name="exchange",
        out_shape=[
            in_vmem((TAB_ROWS, 128), jnp.int32),
            in_vmem((CAP, width, width), f32),
            in_vmem((CAP, width, width), f32),
            in_vmem((CAP, places, rows, width), bf16),
            in_vmem((CAP, width, width), f32),
            in_vmem((CAP, width, width), f32),
        ],
        in_specs=[hbm_spec] * 6,
        out_specs=[vmem_spec] * 6,
        scratch_shapes=[
            pltpu.SMEM((TAB_ROWS, 128), jnp.int32),
            pltpu.VMEM((CAP, width, width), bf16),
            pltpu.VMEM((1, blocks), jnp.int32),
            pltpu.VMEM((blocks, rows, width), bf16),
            pltpu.VMEM((CAP, width, width), bf16),
            pltpu.VMEM((CAP, width, width), bf16),
            pltpu.VMEM((CHUNKS, PIECES, places // 2, rows, part), bf16),
            pltpu.VMEM((CHUNKS, PIECES, places // 2, rows, part), bf16),
            pltpu.VMEM((CAP, devs, rows, width), bf16),
            pltpu.VMEM((width, width), bf16),
            pltpu.VMEM((width, width), f32),
            pltpu.VMEM((width, width), bf16),
            [pltpu.VMEM((places, rows, part), bf16)] * CHUNKS,
            [pltpu.VMEM((places, rows, part), bf16)] * (CHUNKS * three),
            [pltpu.VMEM((devs, rows, (e - b) * width // BACK[-1]), bf16) for b, e in zip(BACK, BACK[1:])],
            dma((7,)),
            dma((CHUNKS, PIECES)),
            dma((CHUNKS, PIECES)),
            dma((CHUNKS, PIECES)),
            dma((CHUNKS, PIECES)),
            dma((CHUNKS,)),
            dma((CHUNKS,)),
            dma((CHUNKS, three)),
            dma((CHUNKS, three)),
            dma((CHUNKS, PIECES)),
            dma((CHUNKS, PIECES)),
            dma((len(BACK) - 1,)),
            dma((len(BACK) - 1,)),
            dma((len(BACK) - 1, PIECES)),
            dma((len(BACK) - 1, PIECES)),
        ],
        compiler_params=pltpu.CompilerParams(
            collective_id=0, has_side_effects=True, vmem_limit_bytes=40 * 2**20
        ),
    )(in_hbm(owner.reshape(1, blocks)), *(in_hbm(x) for x in (gradient, left_factor, right_factor, left_root, right_root)))
    update, left_out, right_out = pl.pallas_call(
        functools.partial(write_out, reps),
        name="write_out",
        out_shape=[
            jax.ShapeDtypeStruct((blocks, rows, width), bf16),
            jax.ShapeDtypeStruct((CAP, width, width), f32),
            jax.ShapeDtypeStruct((CAP, width, width), f32),
        ],
        in_specs=[vmem_spec] * 6,
        out_specs=[hbm_spec] * 3,
        scratch_shapes=[
            pltpu.SMEM((TAB_ROWS, 128), jnp.int32),
            pltpu.VMEM((CAP, width, width), f32),
            pltpu.VMEM((CAP, width, width), f32),
            dma((3,)),
        ],
        compiler_params=pltpu.CompilerParams(vmem_limit_bytes=24 * 2**20),
    )(*(from_vmem(x) for x in (tab, left_gram, right_gram, uall, lf, rf)))
    return update, left_out, right_out


def solution(mesh):
    in_specs = (
        P("rep", None, "dp", None),
        P(),
        P("dp", None, None),
        P("dp", None, None),
        P("dp", None, None),
        P("dp", None, None),
    )
    out_specs = (P(None, "dp", None), P("dp", None, None), P("dp", None, None))
    body = functools.partial(shards, mesh.shape["rep"], mesh.shape["dp"])
    return jax.shard_map(body, mesh=mesh, in_specs=in_specs, out_specs=out_specs, check_vma=False)
```
